32 devices in a mesh: ctx: 8 (over z, x), tab: 4 (over y, core).
Axes of the slice: x: 2, y: 2, z: 4, core: 2. Of those that a mesh axis runs over, the one named last changes fastest.
Arguments:
- table: bfloat16 [8, 4, 4096, 512], P('ctx', 'tab'), may hold values from -6 to 6
- row_ids: int32 [8, 4, 256], P('ctx', 'tab'), may hold values from 0 to 4095
- dests: int32 [8, 4, 4], P('ctx'), may hold values from 0 to 3, as said below
- slots: int32 [8, 4, 4], P('ctx'), may hold values from 0 to 3, as said below
- lengths: int32 [4, 16], P('tab'), may hold values from 1 to 1024, 2048 in all within a row
- tile_mask: int32 [4, 32, 32], P('tab'), may hold values from 0 to 1, as said below
- w_in: bfloat16 [512, 2048], replicated, may hold values from -0.25 to 0.25
- w_out: bfloat16 [512, 512], replicated, may hold values from -0.25 to 0.25
- output_gradient: bfloat16 [4, 2048, 512], P('tab', 'ctx'), may hold values from -6 to 6
Outputs:
- layer_out: bfloat16 [4, 2048, 512], P('tab', 'ctx')
- table_grad: bfloat16 [8, 4, 4096, 512], P('ctx', 'tab')
The draws below stay inside these ranges and needn't reach their ends.
Inputs may be any that keep to these rules, and one draw needn't show every extreme that they name: `dests`: the 4 blocks of one device go to 4 different indices of tab, and every device of a ctx index receives exactly one block for each slot 0 to 3. `slots`: see dests. `lengths`: each row sums to 2048; its longest history has exactly 1024 positions. `tile_mask`: diagonal tiles are 1.
All inputs are finite; a program needn't handle non-finite values.
Results may differ from the reference program's by a relative error of at most 0.012.
Values may be sent and summed in bfloat16 or wider, within the bound.
A program may use at most 192 MiB of HBM per device.

```python
import math
import jax
import jax.numpy as jnp
import numpy as np
from jax import lax

D = 512
H = 4
HD = 128
TAB_ROWS = 4096
BROWS = 64
NBLK = 4
NDOCS = 16
TOK = 256
LEN = 2048
MAXDOC = 1024
NTILE = 32
N_CTX = 8
N_TAB = 4


def routing(key):
    first, second, third = jax.random.split(key, 3)
    offsets = jax.vmap(lambda sub_key: jax.random.permutation(sub_key, N_TAB)[:NBLK])(jax.random.split(first, N_CTX))
    slot_order = jax.vmap(lambda sub_key: jax.random.permutation(sub_key, NBLK))(jax.random.split(second, N_CTX))
    block_order = jax.vmap(lambda sub_key: jax.random.permutation(sub_key, NBLK))(jax.random.split(third, N_CTX * N_TAB))
    block_order = block_order.reshape(N_CTX, N_TAB, NBLK).astype(jnp.int32)
    offset_table = jnp.broadcast_to(offsets[:, None, :].astype(jnp.int32), (N_CTX, N_TAB, NBLK))
    slot_table = jnp.broadcast_to(slot_order[:, None, :].astype(jnp.int32), (N_CTX, N_TAB, NBLK))
    chosen_offset = jnp.take_along_axis(offset_table, block_order, axis=2)
    chosen_slot = jnp.take_along_axis(slot_table, block_order, axis=2)
    sources = jnp.arange(N_TAB, dtype=jnp.int32)[None, :, None]
    destination = (sources + chosen_offset) % N_TAB
    return (destination.astype(jnp.int32), chosen_slot.astype(jnp.int32))


def draw_dests(key, part):
    return routing(key)[0]


def draw_slots(key, part):
    return routing(key)[1]


def draw_tile_mask(key, part):
    key = jax.random.fold_in(key, 7)
    coins = jax.random.randint(key, (N_TAB, NTILE, NTILE), 0, 5)
    diagonal = jnp.eye(NTILE, dtype=jnp.int32)[None, :, :]
    return jnp.maximum((coins < 3).astype(jnp.int32), diagonal).astype(jnp.int32)


def set_ends(values, stream_key, low, high):
    spot = [jax.random.randint(jax.random.fold_in(stream_key, axis), (), 0, length) for axis, length in enumerate(values.shape)]
    longest = values.shape.index(max(values.shape))
    next_to = spot[:longest] + [(spot[longest] + 1) % values.shape[longest]] + spot[longest + 1:]
    return values.at[tuple(spot)].set(low).at[tuple(next_to)].set(high)


def block_levels(rng, extent, cuts, low, largest):
    loudness, own = 1.0, jax.random.fold_in(rng, 6)
    for axis_at, shards_of in cuts:
        heights = jnp.exp(jax.random.uniform(jax.random.fold_in(own, axis_at), (shards_of,), jnp.float32, low / len(cuts), largest / len(cuts)))
        loudness = loudness * jnp.repeat(heights, extent[axis_at] // shards_of).reshape([-1 if axis == axis_at else 1 for axis in range(len(extent))])
    return loudness


def cumulative_ranks(number_of, lean):
    weights = [(1 << 20) // math.isqrt(standing ** lean) + 1 for standing in range(1, number_of + 1)]
    spread = 1 + sum(weights) // (1 << 30)
    return np.cumsum(np.array([max(1, weight // spread) for weight in weights]))


def ranked_ids(key, dims, amount, skew):
    listing = cumulative_ranks(amount, skew)
    lot = jax.random.randint(jax.random.fold_in(key, 1), dims, 0, int(listing[amount - 1]))
    standing = jnp.searchsorted(jnp.asarray(listing, jnp.int32), lot, side="right")
    return jax.random.permutation(jax.random.fold_in(key, 2), amount)[standing].astype(jnp.int32)


def profile(amount, total, most, lean):
    loads = [(1 << 20) // math.isqrt(rank ** lean) + 1 for rank in range(2, amount + 1)]
    spare, counts = total - most - (amount - 1), [1] * (amount - 1)
    while spare > 0:
        movable = [i for i in range(amount - 1) if counts[i] < most]
        whole, budget = sum([loads[i] for i in movable]), spare
        for i in movable:
            extra = min(most - counts[i], max(1, budget * loads[i] // whole), spare)
            counts[i] = counts[i] + extra
            spare = spare - extra
    return np.array([most] + counts)


def uneven_parts(key, amount, total, limit, skew):
    if amount == 2:
        one = jax.random.randint(key, (), max(1, total - limit), min(limit, total - 1) + 1)
        return jnp.stack([one, total - one])
    sizes = jnp.asarray(profile(amount, total, limit, skew), jnp.int32)
    pairs = (amount - 1) // 2
    giver, taker = sizes[1:1 + 2 * pairs:2], sizes[2:2 + 2 * pairs:2]
    margin = jnp.minimum(giver - 1, limit - taker)
    shifted = jax.random.randint(jax.random.fold_in(key, 1), (pairs,), 0, 1 << 20) % (margin + 1)
    sizes = sizes.at[1:1 + 2 * pairs:2].set(giver - shifted).at[2:2 + 2 * pairs:2].set(taker + shifted)
    return sizes[jax.random.permutation(jax.random.fold_in(key, 2), amount)]


def gaussian(stream_key, extent, width, bound, shards=(), held_as=jnp.bfloat16):
    drawn = width * jax.random.normal(stream_key, extent, jnp.float32)
    if shards:
        drawn = drawn * block_levels(stream_key, extent, shards, -0.22, 0.18)
    return jnp.clip(drawn, -bound, bound).astype(held_as)


def setup_inputs(seed: int = 0) -> dict:
    key_list = jax.random.split(jax.random.key(seed), 10)
    table = gaussian(key_list[0], (N_CTX, N_TAB, TAB_ROWS, D), 1.0, 6.0, ((0, 8), (1, 4)))
    row_ids = set_ends(ranked_ids(key_list[1], (N_CTX, N_TAB, TOK), TAB_ROWS, 1), jax.random.fold_in(key_list[1], 3), 0, TAB_ROWS - 1).astype(jnp.int32)
    dests = draw_dests(jax.random.fold_in(key_list[9], 71), 0)
    slots = draw_slots(jax.random.fold_in(key_list[9], 71), 0)
    lengths = jax.vmap(lambda own: uneven_parts(own, NDOCS, LEN, MAXDOC, 2))(jax.random.split(key_list[4], N_TAB)).reshape((N_TAB, NDOCS)).astype(jnp.int32)
    tile_mask = draw_tile_mask(jax.random.fold_in(key_list[9], 71), 0)
    w_in = gaussian(key_list[6], (D, 4 * D), D ** -0.5, 0.25)
    w_out = gaussian(key_list[7], (D, D), D ** -0.5, 0.25)
    output_gradient = gaussian(key_list[8], (N_TAB, LEN, D), 1.0, 6.0, ((0, 4), (1, 8)))
    return {"table": table, "row_ids": row_ids, "dests": dests, "slots": slots, "lengths": lengths, "tile_mask": tile_mask, "w_in": w_in, "w_out": w_out, "output_gradient": output_gradient}


epsilon = 1e-05

def layer_statistics(inputs):
    row_mean = lax.optimization_barrier(jnp.mean(inputs, axis=-1, keepdims=True))
    centred = inputs - row_mean
    inverse = lax.rsqrt(lax.optimization_barrier(jnp.mean(centred * centred, axis=-1, keepdims=True)) + epsilon)
    return (centred * inverse, inverse)

def norm_backward_pass(incoming_gradient, normalized_rows, inverse):
    first = lax.optimization_barrier(jnp.mean(incoming_gradient, axis=-1, keepdims=True))
    second = lax.optimization_barrier(jnp.mean(incoming_gradient * normalized_rows, axis=-1, keepdims=True))
    return inverse * (incoming_gradient - first - normalized_rows * second)

def silu_slope(argument):
    sigmoid_v = jax.nn.sigmoid(argument)
    return sigmoid_v * (1.0 + argument * (1.0 - sigmoid_v))

def rounded(argument):
    return lax.optimization_barrier(argument.astype(jnp.bfloat16)).astype(jnp.float32)

def position_of(stored, rows_dev, chain_count):
    half = rows_dev // 2
    owner = stored // rows_dev
    local = stored % rows_dev
    early = owner * half + local
    late = (2 * chain_count - 1 - owner) * half + local - half
    return jnp.where(local < half, early, late).astype(jnp.int32)

def doc_index(position, doc_ends):
    return lax.optimization_barrier(jnp.sum((position[:, None] >= doc_ends[None, :]).astype(jnp.int32), axis=1))

def allowed_pairs(query_pos, key_pos, doc_ends, tile_table):
    same_doc = doc_index(query_pos, doc_ends)[:, None] == doc_index(key_pos, doc_ends)[None, :]
    causal = key_pos[None, :] <= query_pos[:, None]
    tile_rows = jnp.take(tile_table, query_pos // BROWS, axis=0)
    tile_on = jnp.take(tile_rows, key_pos // BROWS, axis=1) > 0
    return (same_doc & causal & tile_on).astype(jnp.float32)

def group_layer(user_sequence, output_gradient, lengths, tile_table, w_in, w_out):
    score_scale = HD ** (-0.5)
    doc_ends = jnp.cumsum(lengths).astype(jnp.int32)
    centred_scaled_input, inverse_deviation = layer_statistics(user_sequence.astype(jnp.float32))
    normalized_rows = centred_scaled_input.astype(jnp.bfloat16)
    pre = jnp.dot(normalized_rows, w_in, preferred_element_type=jnp.float32)
    act = jax.nn.silu(pre).astype(jnp.bfloat16)
    up_part = act[:, 0:D].astype(jnp.float32)
    value_heads = act[:, D:2 * D].astype(jnp.float32).reshape(LEN, H, HD)
    query_all = act[:, 2 * D:3 * D].astype(jnp.float32)
    key_heads = act[:, 3 * D:4 * D].astype(jnp.float32).reshape(LEN, H, HD)
    key_pos = position_of(jnp.arange(LEN, dtype=jnp.int32), TOK, N_CTX)

    def forward_block(block_index):
        offset = block_index * TOK
        query_pos = position_of(offset + jnp.arange(TOK, dtype=jnp.int32), TOK, N_CTX)
        query_heads = lax.dynamic_slice_in_dim(query_all, offset, TOK, 0).reshape(TOK, H, HD)
        allowed = allowed_pairs(query_pos, key_pos, doc_ends, tile_table)
        scores = jnp.einsum('qhd,khd->hqk', query_heads, key_heads) * score_scale
        probs = rounded(jax.nn.silu(scores) * allowed[None])
        return jnp.einsum('hqk,khd->qhd', probs, value_heads).reshape(TOK, D)
    attn = lax.map(forward_block, jnp.arange(N_CTX, dtype=jnp.int32)).reshape(LEN, D)
    attn_hat, attn_inverse = layer_statistics(attn)
    mixed = (attn_hat * up_part).astype(jnp.bfloat16)
    layer_out = (user_sequence.astype(jnp.float32) + jnp.dot(mixed, w_out, preferred_element_type=jnp.float32)).astype(jnp.bfloat16)
    dmixed = jnp.dot(output_gradient, w_out.T, preferred_element_type=jnp.float32)
    d_up = dmixed * attn_hat
    d_attn = norm_backward_pass(dmixed * up_part, attn_hat, attn_inverse).astype(jnp.bfloat16).astype(jnp.float32)

    def backward_block(running, block_index):
        key_sum, value_sum = running
        offset = block_index * TOK
        query_pos = position_of(offset + jnp.arange(TOK, dtype=jnp.int32), TOK, N_CTX)
        query_heads = lax.dynamic_slice_in_dim(query_all, offset, TOK, 0).reshape(TOK, H, HD)
        grad_heads = lax.dynamic_slice_in_dim(d_attn, offset, TOK, 0).reshape(TOK, H, HD)
        allowed = allowed_pairs(query_pos, key_pos, doc_ends, tile_table)[None]
        scores = jnp.einsum('qhd,khd->hqk', query_heads, key_heads) * score_scale
        probs = rounded(jax.nn.silu(scores) * allowed)
        d_probs = jnp.einsum('qhd,khd->hqk', grad_heads, value_heads)
        d_scores = rounded(d_probs * silu_slope(scores) * allowed * score_scale)
        d_query = jnp.einsum('hqk,khd->qhd', d_scores, key_heads).reshape(TOK, D)
        key_sum = key_sum + jnp.einsum('hqk,qhd->khd', d_scores, query_heads).reshape(LEN, D)
        value_sum = value_sum + jnp.einsum('hqk,qhd->khd', probs, grad_heads).reshape(LEN, D)
        return ((key_sum, value_sum), d_query)
    zero_keys = jnp.zeros((LEN, D), jnp.float32)
    (d_key, d_value), d_query = lax.scan(backward_block, (zero_keys, zero_keys), jnp.arange(N_CTX, dtype=jnp.int32))
    d_query = d_query.reshape(LEN, D)
    d_act = jnp.concatenate([d_up, d_value, d_query, d_key], axis=1)
    d_pre = (d_act * silu_slope(pre)).astype(jnp.bfloat16)
    normalized_gradient = jnp.dot(d_pre, w_in.T, preferred_element_type=jnp.float32)
    sequence_gradient = (output_gradient.astype(jnp.float32) + norm_backward_pass(normalized_gradient, centred_scaled_input, inverse_deviation)).astype(jnp.bfloat16)
    return (layer_out, sequence_gradient)

def reference(table, row_ids, dests, slots, lengths, tile_mask, w_in, w_out, output_gradient):
    looked = jax.vmap(jax.vmap(lambda shard_rows, shard_ids: jnp.take(shard_rows, shard_ids, axis=0)))(table, row_ids)
    blocks = looked.reshape(N_CTX, N_TAB, NBLK, BROWS, D)
    ctx_index = jnp.broadcast_to(jnp.arange(N_CTX, dtype=jnp.int32)[:, None, None], dests.shape)
    placed = jnp.zeros((N_TAB, N_CTX, NBLK, BROWS, D), table.dtype).at[dests, ctx_index, slots].set(blocks)
    user_sequence = placed.reshape(N_TAB, LEN, D)

    def one_group(group_args):
        return group_layer(group_args[0], group_args[1], group_args[2], group_args[3], w_in, w_out)
    layer_out, sequence_gradient = lax.map(one_group, (user_sequence, output_gradient, lengths, tile_mask))
    returned = sequence_gradient.reshape(N_TAB, N_CTX, NBLK, BROWS, D)[dests, ctx_index, slots]
    returned = returned.reshape(N_CTX * N_TAB, TOK, D)
    flat_ids = row_ids.reshape(N_CTX * N_TAB, TOK)

    def table_rows(pair_args):
        grads, shard_ids = pair_args
        summed = jnp.zeros((TAB_ROWS, D), jnp.float32).at[shard_ids].add(grads.astype(jnp.float32))
        return summed.astype(jnp.bfloat16)
    table_grad = lax.map(table_rows, (returned, flat_ids)).reshape(N_CTX, N_TAB, TAB_ROWS, D)
    return (layer_out, table_grad)
```

```python
import functools

import jax
import jax.numpy as jnp
from jax import lax
from jax.experimental import pallas as pl
from jax.experimental.pallas import tpu as pltpu
from jax.sharding import PartitionSpec as P

H = 4
BROWS = 64
NBLK = 4
FAST = 2

epsilon = 1e-05
MESH = pl.DeviceIdType.MESH
NT = (((1,), (1,)), ((), ()))
TN = (((0,), (0,)), ((), ()))


def dot(a, b):
    return jnp.dot(a, b, preferred_element_type=jnp.float32)


def dot_nt(a, b):
    return lax.dot_general(a, b, NT, preferred_element_type=jnp.float32)


def layer_statistics(inputs):
    row_mean = jnp.mean(inputs, axis=-1, keepdims=True)
    centred = inputs - row_mean
    inverse = lax.rsqrt(jnp.mean(centred * centred, axis=-1, keepdims=True) + epsilon)
    return (centred * inverse, inverse)


def norm_backward_pass(incoming, normalized, inverse):
    first = jnp.mean(incoming, axis=-1, keepdims=True)
    second = jnp.mean(incoming * normalized, axis=-1, keepdims=True)
    return inverse * (incoming - first - normalized * second)


def silu_half(half):
    return half * (1.0 + jnp.tanh(half))


def slope_half(half, tanh):
    return (0.5 + 0.5 * tanh) * (1.0 + half * (1.0 - tanh))


def lookup_kernel(ids_ref, table_ref, out_ref, acc):
    step = pl.program_id(0)
    rows = table_ref.shape[2]
    count = ids_ref.shape[2]

    @pl.when(step == 0)
    def _():
        acc[...] = jnp.zeros_like(acc)

    base = step * rows
    row = lax.broadcasted_iota(jnp.int32, (rows, count), 0) + base
    pick = jnp.where(row == ids_ref[0], 1.0, 0.0).astype(jnp.bfloat16)
    acc[...] += lax.dot_general(
        pick, table_ref[0, 0], TN, preferred_element_type=jnp.float32
    )

    @pl.when(step == pl.num_programs(0) - 1)
    def _():
        out_ref[...] = acc[...].astype(out_ref.dtype)


def scatter_kernel(ids_ref, grads_ref, out_ref):
    rows = out_ref.shape[2]
    count = ids_ref.shape[2]
    row = lax.broadcasted_iota(jnp.int32, (rows, count), 0) + pl.program_id(0) * rows
    pick = jnp.where(row == ids_ref[0], 1.0, 0.0).astype(jnp.bfloat16)
    out_ref[0, 0] = dot(pick, grads_ref[...]).astype(out_ref.dtype)


def layer_kernel(
    n,
    tabs,
    dests,
    slots,
    lengths,
    tiles,
    rows_ref,
    w_in,
    w_out,
    og_ref,
    out_ref,
    grads_ref,
    xg,
    dg,
    vqk,
    gq,
    pk,
    gk,
    pre,
    attn,
    seq,
    dq,
    dk,
    dv,
    dup,
    startq,
    route_out,
    route_in,
    back_out,
    back_in,
    xs,
    xr,
    ds_,
    dr,
    rs,
    rr,
    bs,
    br,
):
    me = lax.axis_index("ctx")
    tab = lax.axis_index("tab")
    levels = n // FAST
    z = me // FAST
    x = me % FAST
    rows = rows_ref.shape[0]
    width = rows_ref.shape[1]
    half = rows // 2
    per_half = half // BROWS
    hd = width // H
    scale = hd ** (-0.5)

    barrier = pltpu.get_barrier_semaphore()

    def greet_ctx(k, carry):
        pl.semaphore_signal(
            barrier, inc=1, device_id=(lax.rem(me + k, n), tab), device_id_type=MESH
        )
        return carry

    def greet_tab(k, carry):
        pl.semaphore_signal(
            barrier, inc=1, device_id=(me, lax.rem(tab + k, tabs)), device_id_type=MESH
        )
        return carry

    lax.fori_loop(1, n, greet_ctx, 0)
    lax.fori_loop(1, tabs, greet_tab, 0)

    def choose(hit, block, other):
        on = jnp.full(block.shape, hit.astype(jnp.int32)) > 0
        return jnp.where(on, block, other)

    def block_for(t):
        block = rows_ref[0:BROWS, :]
        for p in range(1, NBLK):
            other = rows_ref[p * BROWS : (p + 1) * BROWS, :]
            block = choose(dests[0, tab, p] == t, other, block)
        return block

    def route_copy(src, dst, send, recv, t):
        return pltpu.make_async_remote_copy(
            src_ref=src.at[t],
            dst_ref=dst.at[tab],
            send_sem=send.at[t],
            recv_sem=recv.at[tab],
            device_id=(me, t),
            device_id_type=MESH,
        )

    def route_wait(src, dst, send, recv, t):
        pltpu.make_async_remote_copy(
            src_ref=src.at[t],
            dst_ref=dst.at[t],
            send_sem=send.at[t],
            recv_sem=recv.at[t],
            device_id=(me, t),
            device_id_type=MESH,
        ).wait()

    for k in range(tabs):
        t = lax.rem(tab + k, tabs)
        if k == 0:
            route_in[tab] = block_for(t)
        else:
            route_out[t] = block_for(t)

    pl.semaphore_wait(barrier, n + tabs - 2)

    for k in range(1, tabs):
        route_copy(route_out, route_in, rs, rr, lax.rem(tab + k, tabs)).start()

    def starts_of(pos):
        end = jnp.int32(0)
        start = jnp.zeros_like(pos)
        for e in range(lengths.shape[1]):
            end = end + lengths[0, e]
            start = jnp.where(pos >= end, end, start)
        return start

    def positions(s, shape, dim):
        local = lax.broadcasted_iota(jnp.int32, shape, dim)
        return local + jnp.where(local < half, s * half, (2 * n - 1 - s) * half - half)

    startq[...] = starts_of(positions(me, (rows, 128), 0))
    attn[...] = jnp.zeros_like(attn)

    def tile_id(s, a):
        if a < per_half:
            return s * per_half + a
        return (2 * n - 1 - s) * per_half + a - per_half

    count = 2 * per_half

    def tile_rows(pick):
        block = lax.broadcasted_iota(jnp.int32, (BROWS, rows), 1) // BROWS
        stripes = []
        for a in range(count):
            line = jnp.zeros((BROWS, rows), jnp.int32)
            for b in range(count):
                line = jnp.where(block == b, pick(a, b), line)
            stripes.append(line)
        return jnp.concatenate(stripes, axis=0) > 0

    def query_mask(s):
        own = positions(me, (rows, rows), 0)
        other = positions(s, (rows, rows), 1)
        first = jnp.broadcast_to(startq[:, 0:1], (rows, rows))
        on = tile_rows(lambda a, b: tiles[0, tile_id(me, a), tile_id(s, b)])
        return jnp.where((other <= own) & (other >= first) & on, 1.0, 0.0)

    def key_mask(s):
        own = positions(me, (rows, rows), 0)
        other = positions(s, (rows, rows), 1)
        first = starts_of(positions(s, (1, rows), 1))
        on = tile_rows(lambda a, b: tiles[0, tile_id(s, b), tile_id(me, a)])
        return jnp.where((own <= other) & (own >= first) & on, 1.0, 0.0)

    def take(buf, part, s, h):
        return buf[part, s, :, h * hd : (h + 1) * hd]

    def project(s):
        block = xg[s]
        for part in range(3):
            lo = (part + 1) * width
            value = dot(block, w_in[:, lo : lo + width])
            vqk[part, s] = silu_half(0.5 * value).astype(jnp.bfloat16)

    def forward(s):
        project(s)
        mask = query_mask(s)
        for h in range(H):
            cut = slice(h * hd, (h + 1) * hd)
            halfs = dot_nt(take(vqk, 1, me, h), take(vqk, 2, s, h)) * (0.5 * scale)
            tanh = jnp.tanh(halfs)
            probs = (halfs * (1.0 + tanh) * mask).astype(jnp.bfloat16)
            gq[s, h] = (slope_half(halfs, tanh) * (mask * scale)).astype(jnp.bfloat16)
            attn[:, cut] += dot(probs, take(vqk, 0, s, h))
        mask = key_mask(s)
        for h in range(H):
            halfs = dot_nt(take(vqk, 2, me, h), take(vqk, 1, s, h)) * (0.5 * scale)
            tanh = jnp.tanh(halfs)
            pk[s, h] = (halfs * (1.0 + tanh) * mask).astype(jnp.bfloat16)
            gk[s, h] = (slope_half(halfs, tanh) * (mask * scale)).astype(jnp.bfloat16)

    def query_back(s):
        for h in range(H):
            cut = slice(h * hd, (h + 1) * hd)
            slope = gq[s, h].astype(jnp.float32)
            dsc = dot_nt(dg[me, :, cut], take(vqk, 0, s, h)) * slope
            dq[:, cut] += dot(dsc.astype(jnp.bfloat16), take(vqk, 2, s, h))

    def key_back(s):
        for h in range(H):
            cut = slice(h * hd, (h + 1) * hd)
            grad = dg[s, :, cut]
            slope = gk[s, h].astype(jnp.float32)
            dsc = dot_nt(take(vqk, 0, me, h), grad) * slope
            dk[:, cut] += dot(dsc.astype(jnp.bfloat16), take(vqk, 1, s, h))
            dv[:, cut] += dot(pk[s, h], grad)

    def gather(buf, send, recv, compute, filler):
        def copy(s, way):
            to = (me - FAST, me + FAST, z * FAST + (FAST - 1 - x))[way]
            return pltpu.make_async_remote_copy(
                src_ref=buf.at[s],
                dst_ref=buf.at[s],
                send_sem=send.at[way, s],
                recv_sem=recv.at[s],
                device_id=(to, tab),
                device_id_type=MESH,
            )

        def ways(zz, action):
            s = zz * FAST + x

            @pl.when((zz >= z) & (z > 0))
            def _():
                action(copy(s, 0))

            @pl.when((zz <= z) & (z < levels - 1))
            def _():
                action(copy(s, 1))

            action(copy(s, 2))

        def level(j):
            far = (j + 1) // 2
            return z + jnp.where(j % 2 == 1, -far, far)

        def step(j, carry):
            zz = level(j)

            @pl.when((j < 2 * levels - 1) & (zz >= 0) & (zz < levels))
            def _():
                s = zz * FAST + x

                @pl.when(j > 0)
                def _():
                    copy(s, 2).wait_recv()

                ways(zz, lambda c: c.start())
                compute(s)

            if filler is not None:
                filler(j)
            before = level(j - 1)

            @pl.when((j > 0) & (before >= 0) & (before < levels))
            def _():
                s = before * FAST + (FAST - 1 - x)
                copy(s, 2).wait_recv()
                compute(s)

            return carry

        lax.fori_loop(0, 2 * levels, step, 0)

        def drain(zz, carry):
            ways(zz, lambda c: c.wait_send())
            return carry

        lax.fori_loop(0, levels, drain, 0)

    for k in range(1, tabs):
        route_wait(route_out, route_in, rs, rr, lax.rem(tab + k, tabs))

    def arrives(s, t):
        count = jnp.int32(0)
        for p in range(NBLK):
            hit = (dests[0, t, p] == tab) & (slots[0, t, p] == s)
            count += hit.astype(jnp.int32)
        return count > 0

    for s in range(NBLK):
        block = route_in[0]
        for t in range(1, tabs):
            block = choose(arrives(s, t), route_in[t], block)
        seq[s * BROWS : (s + 1) * BROWS, :] = block

    xhat, inverse = layer_statistics(seq[...].astype(jnp.float32))
    xg[me] = xhat.astype(jnp.bfloat16)

    gather(xg, xs, xr, forward, None)

    for part in range(4):
        pre[part] = 0.5 * dot(xg[me], w_in[:, part * width : (part + 1) * width])
    up = silu_half(pre[0]).astype(jnp.bfloat16).astype(jnp.float32)
    attn_hat, attn_inverse = layer_statistics(attn[...])
    dmixed = dot_nt(og_ref[0], w_out[...])
    dup[...] = dmixed * attn_hat
    dg[me] = norm_backward_pass(dmixed * up, attn_hat, attn_inverse).astype(jnp.bfloat16)
    mixed = (attn_hat * up).astype(jnp.bfloat16)
    out_ref[0] = (seq[...].astype(jnp.float32) + dot(mixed, w_out[...])).astype(
        jnp.bfloat16
    )
    dq[...] = jnp.zeros_like(dq)
    dk[...] = jnp.zeros_like(dk)
    dv[...] = jnp.zeros_like(dv)

    gather(dg, ds_, dr, key_back, query_back)

    def d_pre(part, grad):
        halfs = pre[part]
        return (grad * slope_half(halfs, jnp.tanh(halfs))).astype(jnp.bfloat16)

    normalized = jnp.zeros((rows, width), jnp.float32)
    for part, grad in enumerate((dup, dv, dq, dk)):
        piece = d_pre(part, grad[...])
        normalized += dot_nt(piece, w_in[:, part * width : (part + 1) * width])
    xhat, inverse = layer_statistics(seq[...].astype(jnp.float32))
    attn[...] = og_ref[0].astype(jnp.float32) + norm_backward_pass(
        normalized, xhat, inverse
    )

    def back_block(t):
        block = attn[0:BROWS, :]
        for s in range(1, NBLK):
            other = attn[s * BROWS : (s + 1) * BROWS, :]
            block = choose(arrives(s, t), other, block)
        return block.astype(jnp.bfloat16)

    for k in range(tabs):
        t = lax.rem(tab + k, tabs)
        if k == 0:
            back_in[tab] = back_block(t)
        else:
            back_out[t] = back_block(t)
            route_copy(back_out, back_in, bs, br, t).start()
    for k in range(1, tabs):
        route_wait(back_out, back_in, bs, br, lax.rem(tab + k, tabs))
    for p in range(NBLK):
        block = back_in[0]
        for t in range(1, tabs):
            block = choose(dests[0, tab, p] == t, back_in[t], block)
        grads_ref[p * BROWS : (p + 1) * BROWS, :] = block


def body(n, tabs, table, row_ids, dests, slots, lengths, tile_mask, w_in, w_out, og):
    count = row_ids.shape[2]
    width = w_out.shape[0]
    table_rows = table.shape[2]
    cut = 512
    bf16, f32 = jnp.bfloat16, jnp.float32
    vmem = pl.BlockSpec(memory_space=pltpu.VMEM)
    smem = pl.BlockSpec(memory_space=pltpu.SMEM)
    ids_spec = pl.BlockSpec((1, 1, count), lambda i: (0, 0, 0))
    tile_spec = pl.BlockSpec((1, 1, cut, width), lambda i: (0, 0, i, 0))
    rows_spec = pl.BlockSpec((count, width), lambda i: (0, 0))
    looked = pl.pallas_call(
        lookup_kernel,
        out_shape=jax.ShapeDtypeStruct((count, width), bf16),
        grid=(table_rows // cut,),
        in_specs=[ids_spec, tile_spec],
        out_specs=rows_spec,
        scratch_shapes=[pltpu.VMEM((count, width), f32)],
        name="lookup",
    )(row_ids, table)
    dma = pltpu.SemaphoreType.DMA
    layer_out, row_grads = pl.pallas_call(
        functools.partial(layer_kernel, n, tabs),
        out_shape=(
            jax.ShapeDtypeStruct((1, count, width), bf16),
            jax.ShapeDtypeStruct((count, width), bf16),
        ),
        in_specs=[smem] * 4 + [vmem] * 4,
        out_specs=(vmem, vmem),
        scratch_shapes=[
            pltpu.VMEM((n, count, width), bf16),
            pltpu.VMEM((n, count, width), bf16),
            pltpu.VMEM((3, n, count, width), bf16),
            pltpu.VMEM((n, H, count, count), bf16),
            pltpu.VMEM((n, H, count, count), bf16),
            pltpu.VMEM((n, H, count, count), bf16),
            pltpu.VMEM((4, count, width), f32),
            pltpu.VMEM((count, width), f32),
            pltpu.VMEM((count, width), bf16),
            pltpu.VMEM((count, width), f32),
            pltpu.VMEM((count, width), f32),
            pltpu.VMEM((count, width), f32),
            pltpu.VMEM((count, width), f32),
            pltpu.VMEM((count, 128), jnp.int32),
            pltpu.VMEM((tabs, BROWS, width), bf16),
            pltpu.VMEM((tabs, BROWS, width), bf16),
            pltpu.VMEM((tabs, BROWS, width), bf16),
            pltpu.VMEM((tabs, BROWS, width), bf16),
            dma((3, n)),
            dma((n,)),
            dma((3, n)),
            dma((n,)),
            dma((tabs,)),
            dma((tabs,)),
            dma((tabs,)),
            dma((tabs,)),
        ],
        compiler_params=pltpu.CompilerParams(
            collective_id=0, has_side_effects=True, vmem_limit_bytes=60 * 1024 * 1024
        ),
        name="layer",
    )(dests, slots, lengths, tile_mask, looked, w_in, w_out, og)
    table_grad = pl.pallas_call(
        scatter_kernel,
        out_shape=jax.ShapeDtypeStruct((1, 1, table_rows, width), bf16),
        grid=(table_rows // cut,),
        in_specs=[ids_spec, rows_spec],
        out_specs=tile_spec,
        name="table_grad",
    )(row_ids, row_grads)
    return layer_out, table_grad


def solution(mesh):
    in_specs = (
        P("ctx", "tab", None, None),
        P("ctx", "tab", None),
        P("ctx", None, None),
        P("ctx", None, None),
        P("tab", None),
        P("tab", None, None),
        P(),
        P(),
        P("tab", "ctx", None),
    )
    out_specs = (P("tab", "ctx", None), P("ctx", "tab", None, None))
    return jax.shard_map(
        functools.partial(body, mesh.shape["ctx"], mesh.shape["tab"]),
        mesh=mesh,
        in_specs=in_specs,
        out_specs=out_specs,
        check_vma=False,
    )
```

```python
import functools

import jax
import jax.numpy as jnp
from jax import lax
from jax.experimental import pallas as pl
from jax.experimental.pallas import tpu as pltpu
from jax.sharding import PartitionSpec as P

H = 4
BROWS = 64
NBLK = 4
FAST = 2

epsilon = 1e-05
MESH = pl.DeviceIdType.MESH
NT = (((1,), (1,)), ((), ()))
TN = (((0,), (0,)), ((), ()))


def dot(a, b):
    return jnp.dot(a, b, preferred_element_type=jnp.float32)


def dot_nt(a, b):
    return lax.dot_general(a, b, NT, preferred_element_type=jnp.float32)


def layer_statistics(inputs):
    row_mean = jnp.mean(inputs, axis=-1, keepdims=True)
    centred = inputs - row_mean
    inverse = lax.rsqrt(jnp.mean(centred * centred, axis=-1, keepdims=True) + epsilon)
    return (centred * inverse, inverse)


def norm_backward_pass(incoming, normalized, inverse):
    first = jnp.mean(incoming, axis=-1, keepdims=True)
    second = jnp.mean(incoming * normalized, axis=-1, keepdims=True)
    return inverse * (incoming - first - normalized * second)


def silu_half(half):
    return half * (1.0 + jnp.tanh(half))


def slope_half(half, tanh):
    return (0.5 + 0.5 * tanh) * (1.0 + half * (1.0 - tanh))


def lookup_kernel(ids_ref, table_ref, out_ref, acc, column):
    step = pl.program_id(0)
    rows = table_ref.shape[2]
    count = ids_ref.shape[2]

    @pl.when(step == 0)
    def _():
        acc[...] = jnp.zeros_like(acc)
        line = jnp.broadcast_to(ids_ref[0].astype(jnp.float32), (128, count))
        column[...] = line.T.astype(jnp.int32)

    lane = lax.broadcasted_iota(jnp.int32, (count, 128), 1) + step * rows
    picks = [
        jnp.where(column[...] == lane + k * 128, 1.0, 0.0).astype(jnp.bfloat16)
        for k in range(rows // 128)
    ]
    acc[...] += dot(jnp.concatenate(picks, axis=1), table_ref[0, 0])

    @pl.when(step == pl.num_programs(0) - 1)
    def _():
        out_ref[...] = acc[...].astype(out_ref.dtype)


def scatter_kernel(ids_ref, grads_ref, out_ref):
    rows = out_ref.shape[2]
    count = ids_ref.shape[2]
    row = lax.broadcasted_iota(jnp.int32, (rows, count), 0) + pl.program_id(0) * rows
    pick = jnp.where(row == ids_ref[0], 1.0, 0.0).astype(jnp.bfloat16)
    out_ref[0, 0] = dot(pick, grads_ref[...]).astype(out_ref.dtype)


def layer_kernel(
    n,
    tabs,
    dests,
    slots,
    lengths,
    tiles,
    rows_ref,
    w_in,
    w_out,
    og_ref,
    out_ref,
    grads_ref,
    xg,
    dg,
    vqk,
    gq,
    pk,
    gk,
    pre,
    attn,
    seq,
    dq,
    dk,
    dv,
    dup,
    dm,
    up,
    xhat,
    xinv,
    startq,
    route_out,
    route_in,
    back_out,
    back_in,
    xs,
    xr,
    ds_,
    dr,
    rs,
    rr,
    bs,
    br,
):
    me = lax.axis_index("ctx")
    tab = lax.axis_index("tab")
    levels = n // FAST
    z = me // FAST
    x = me % FAST
    rows = rows_ref.shape[0]
    width = rows_ref.shape[1]
    half = rows // 2
    per_half = half // BROWS
    hd = width // H
    scale = hd ** (-0.5)

    barrier = pltpu.get_barrier_semaphore()

    def greet_ctx(k, carry):
        pl.semaphore_signal(
            barrier, inc=1, device_id=(lax.rem(me + k, n), tab), device_id_type=MESH
        )
        return carry

    def greet_tab(k, carry):
        pl.semaphore_signal(
            barrier, inc=1, device_id=(me, lax.rem(tab + k, tabs)), device_id_type=MESH
        )
        return carry

    lax.fori_loop(1, n, greet_ctx, 0)
    lax.fori_loop(1, tabs, greet_tab, 0)

    def choose(hit, block, other):
        on = jnp.full(block.shape, hit.astype(jnp.int32)) > 0
        return jnp.where(on, block, other)

    def block_for(t):
        block = rows_ref[0:BROWS, :]
        for p in range(1, NBLK):
            other = rows_ref[p * BROWS : (p + 1) * BROWS, :]
            block = choose(dests[0, tab, p] == t, other, block)
        return block

    def route_copy(src, dst, send, recv, t):
        return pltpu.make_async_remote_copy(
            src_ref=src.at[t],
            dst_ref=dst.at[tab],
            send_sem=send.at[t],
            recv_sem=recv.at[tab],
            device_id=(me, t),
            device_id_type=MESH,
        )

    def route_wait(src, dst, send, recv, t):
        pltpu.make_async_remote_copy(
            src_ref=src.at[t],
            dst_ref=dst.at[t],
            send_sem=send.at[t],
            recv_sem=recv.at[t],
            device_id=(me, t),
            device_id_type=MESH,
        ).wait()

    for k in range(tabs):
        t = lax.rem(tab + k, tabs)
        if k == 0:
            route_in[tab] = block_for(t)
        else:
            route_out[t] = block_for(t)

    pl.semaphore_wait(barrier, n + tabs - 2)

    for k in range(1, tabs):
        route_copy(route_out, route_in, rs, rr, lax.rem(tab + k, tabs)).start()

    dm[...] = dot_nt(og_ref[0], w_out[...])

    def starts_of(pos):
        end = jnp.int32(0)
        start = jnp.zeros_like(pos)
        for e in range(lengths.shape[1]):
            end = end + lengths[0, e]
            start = jnp.where(pos >= end, end, start)
        return start

    def base_of(s, side):
        return (2 * n - 1 - s) * half if side else s * half

    for side in range(2):
        local = lax.broadcasted_iota(jnp.int32, (half, 128), 0)
        startq[side * half : (side + 1) * half, :] = starts_of(local + base_of(me, side))
    attn[...] = jnp.zeros_like(attn)

    def tile_rows(pick):
        block = lax.broadcasted_iota(jnp.int32, (BROWS, half), 1) // BROWS
        stripes = []
        for a in range(per_half):
            line = jnp.full((BROWS, half), pick(a, 0))
            for b in range(1, per_half):
                line = jnp.where(block == b, pick(a, b), line)
            stripes.append(line)
        return jnp.concatenate(stripes, axis=0) > 0

    def query_mask(s, mine, theirs):
        at, to = base_of(me, mine), base_of(s, theirs)
        own = lax.broadcasted_iota(jnp.int32, (half, half), 0) + at
        other = lax.broadcasted_iota(jnp.int32, (half, half), 1) + to
        first = startq[mine * half : (mine + 1) * half, :]
        at, to = at // BROWS, to // BROWS
        on = tile_rows(lambda a, b: tiles[0, at + a, to + b])
        return jnp.where((other <= own) & (other >= first) & on, 1.0, 0.0)

    def key_mask(s, mine, theirs):
        at, to = base_of(me, mine), base_of(s, theirs)
        own = lax.broadcasted_iota(jnp.int32, (half, half), 0) + at
        other = lax.broadcasted_iota(jnp.int32, (half, half), 1) + to
        first = starts_of(lax.broadcasted_iota(jnp.int32, (1, half), 1) + to)
        at, to = at // BROWS, to // BROWS
        on = tile_rows(lambda a, b: tiles[0, to + b, at + a])
        return jnp.where((own <= other) & (own >= first) & on, 1.0, 0.0)

    def side_rows(side):
        return slice(side * half, (side + 1) * half)

    def take(part, s, side, h):
        return vqk[part, s, side_rows(side), h * hd : (h + 1) * hd]

    def project(s):
        block = xg[s]
        for part in range(3):
            lo = (part + 1) * width
            value = dot(block, w_in[:, lo : lo + width])
            vqk[part, s] = silu_half(0.5 * value).astype(jnp.bfloat16)

    def quads(s):
        return (
            (s <= me, 0, 0, 1, 1),
            (s >= n - 1 - me, 1, 0, 0, 1),
            (s >= me, 1, 1, 0, 0),
        )

    def forward(s):
        project(s)
        for i, (when, qm, kt, km, qt) in enumerate(quads(s)):

            @pl.when(when)
            def _(i=i, qm=qm, kt=kt, km=km, qt=qt):
                mask = query_mask(s, qm, kt)
                scaled = mask * scale
                mask_k = key_mask(s, km, qt)
                scaled_k = mask_k * scale
                for h in range(H):
                    cut = slice(h * hd, (h + 1) * hd)
                    halfs = dot_nt(take(1, me, qm, h), take(2, s, kt, h)) * (0.5 * scale)
                    tanh = jnp.tanh(halfs)
                    probs = (halfs * (1.0 + tanh) * mask).astype(jnp.bfloat16)
                    gq[i, s, h] = (slope_half(halfs, tanh) * scaled).astype(jnp.bfloat16)
                    attn[side_rows(qm), cut] += dot(probs, take(0, s, kt, h))
                    halfs = dot_nt(take(2, me, km, h), take(1, s, qt, h)) * (0.5 * scale)
                    tanh = jnp.tanh(halfs)
                    pk[i, s, h] = (halfs * (1.0 + tanh) * mask_k).astype(jnp.bfloat16)
                    gk[i, s, h] = (slope_half(halfs, tanh) * scaled_k).astype(jnp.bfloat16)

    def query_back(s):
        for i, (when, qm, kt, _, _) in enumerate(quads(s)):

            @pl.when(when)
            def _(i=i, qm=qm, kt=kt):
                for h in range(H):
                    cut = slice(h * hd, (h + 1) * hd)
                    slope = gq[i, s, h].astype(jnp.float32)
                    dsc = dot_nt(dg[me, side_rows(qm), cut], take(0, s, kt, h)) * slope
                    dq[side_rows(qm), cut] += dot(
                        dsc.astype(jnp.bfloat16), take(2, s, kt, h)
                    )

    def key_back(s):
        for i, (when, _, _, km, qt) in enumerate(quads(s)):

            @pl.when(when)
            def _(i=i, km=km, qt=qt):
                for h in range(H):
                    cut = slice(h * hd, (h + 1) * hd)
                    grad = dg[s, side_rows(qt), cut]
                    slope = gk[i, s, h].astype(jnp.float32)
                    dsc = dot_nt(take(0, me, km, h), grad) * slope
                    dk[side_rows(km), cut] += dot(
                        dsc.astype(jnp.bfloat16), take(1, s, qt, h)
                    )
                    dv[side_rows(km), cut] += dot(pk[i, s, h], grad)

    def gather(buf, send, recv, compute, filler):
        def copy(s, way):
            to = (me - FAST, me + FAST, z * FAST + (FAST - 1 - x))[way]
            return pltpu.make_async_remote_copy(
                src_ref=buf.at[s],
                dst_ref=buf.at[s],
                send_sem=send.at[way, s],
                recv_sem=recv.at[s],
                device_id=(to, tab),
                device_id_type=MESH,
            )

        def ways(zz, action):
            s = zz * FAST + x

            @pl.when((zz >= z) & (z > 0))
            def _():
                action(copy(s, 0))

            @pl.when((zz <= z) & (z < levels - 1))
            def _():
                action(copy(s, 1))

            action(copy(s, 2))

        def level(j):
            far = (j + 1) // 2
            return z + jnp.where(j % 2 == 1, -far, far)

        def step(j, carry):
            zz = level(j)

            @pl.when((j < 2 * levels - 1) & (zz >= 0) & (zz < levels))
            def _():
                s = zz * FAST + x

                @pl.when(j > 0)
                def _():
                    copy(s, 2).wait_recv()

                ways(zz, lambda c: c.start())
                compute(s)

            filler(j)
            before = level(j - 1)

            @pl.when((j > 0) & (before >= 0) & (before < levels))
            def _():
                s = before * FAST + (FAST - 1 - x)
                copy(s, 2).wait_recv()
                compute(s)

            return carry

        lax.fori_loop(0, 2 * levels, step, 0)

        def drain(zz, carry):
            ways(zz, lambda c: c.wait_send())
            return carry

        lax.fori_loop(0, levels, drain, 0)

    for k in range(1, tabs):
        route_wait(route_out, route_in, rs, rr, lax.rem(tab + k, tabs))

    def arrives(s, t):
        count = jnp.int32(0)
        for p in range(NBLK):
            hit = (dests[0, t, p] == tab) & (slots[0, t, p] == s)
            count += hit.astype(jnp.int32)
        return count > 0

    for s in range(NBLK):
        block = route_in[0]
        for t in range(1, tabs):
            block = choose(arrives(s, t), route_in[t], block)
        seq[s * BROWS : (s + 1) * BROWS, :] = block

    normal, inverse = layer_statistics(seq[...].astype(jnp.float32))
    xg[me] = normal.astype(jnp.bfloat16)
    xhat[...] = normal
    xinv[...] = jnp.broadcast_to(inverse, xinv.shape)

    def part_of(part):
        return w_in[:, part * width : (part + 1) * width]

    def own_rows(j):
        @pl.when(j == 0)
        def _():
            for part in range(4):
                halfs = 0.5 * dot(xg[me], part_of(part))
                tanh = jnp.tanh(halfs)
                pre[part] = slope_half(halfs, tanh)
                if part == 0:
                    act = (halfs * (1.0 + tanh)).astype(jnp.bfloat16)
                    up[...] = act.astype(jnp.float32)

    gather(xg, xs, xr, forward, own_rows)

    attn_hat, attn_inverse = layer_statistics(attn[...])
    dg[me] = norm_backward_pass(dm[...] * up[...], attn_hat, attn_inverse).astype(
        jnp.bfloat16
    )
    attn[...] = attn_hat
    dq[...] = jnp.zeros_like(dq)
    dk[...] = jnp.zeros_like(dk)
    dv[...] = jnp.zeros_like(dv)

    def d_pre(part, grad):
        return dot_nt((grad * pre[part]).astype(jnp.bfloat16), part_of(part))

    def own_back(j):
        @pl.when(j == 0)
        def _():
            attn_hat = attn[...]
            mixed = (attn_hat * up[...]).astype(jnp.bfloat16)
            out_ref[0] = (seq[...].astype(jnp.float32) + dot(mixed, w_out[...])).astype(
                jnp.bfloat16
            )
            dup[...] = d_pre(0, dm[...] * attn_hat)

        for k in range(n // (2 * levels)):
            query_back(j * (n // (2 * levels)) + k)

        @pl.when(j == 2 * levels - 1)
        def _():
            dup[...] += d_pre(2, dq[...])

    gather(dg, ds_, dr, key_back, own_back)

    normalized = dup[...] + d_pre(1, dv[...]) + d_pre(3, dk[...])
    attn[...] = og_ref[0].astype(jnp.float32) + norm_backward_pass(
        normalized, xhat[...], xinv[:, 0:1]
    )

    def back_block(t):
        block = attn[0:BROWS, :]
        for s in range(1, NBLK):
            other = attn[s * BROWS : (s + 1) * BROWS, :]
            block = choose(arrives(s, t), other, block)
        return block.astype(jnp.bfloat16)

    for k in range(tabs):
        t = lax.rem(tab + k, tabs)
        if k == 0:
            back_in[tab] = back_block(t)
        else:
            back_out[t] = back_block(t)
            route_copy(back_out, back_in, bs, br, t).start()
    for k in range(1, tabs):
        route_wait(back_out, back_in, bs, br, lax.rem(tab + k, tabs))
    for p in range(NBLK):
        block = back_in[0]
        for t in range(1, tabs):
            block = choose(dests[0, tab, p] == t, back_in[t], block)
        grads_ref[p * BROWS : (p + 1) * BROWS, :] = block


def body(n, tabs, table, row_ids, dests, slots, lengths, tile_mask, w_in, w_out, og):
    count = row_ids.shape[2]
    width = w_out.shape[0]
    table_rows = table.shape[2]
    cut = 1024
    bf16, f32 = jnp.bfloat16, jnp.float32
    vmem = pl.BlockSpec(memory_space=pltpu.VMEM)
    smem = pl.BlockSpec(memory_space=pltpu.SMEM)
    ids_spec = pl.BlockSpec((1, 1, count), lambda i: (0, 0, 0))
    tile_spec = pl.BlockSpec((1, 1, cut, width), lambda i: (0, 0, i, 0))
    rows_spec = pl.BlockSpec((count, width), lambda i: (0, 0))
    looked = pl.pallas_call(
        lookup_kernel,
        out_shape=jax.ShapeDtypeStruct((count, width), bf16),
        grid=(table_rows // cut,),
        in_specs=[ids_spec, tile_spec],
        out_specs=rows_spec,
        scratch_shapes=[
            pltpu.VMEM((count, width), f32),
            pltpu.VMEM((count, 128), jnp.int32),
        ],
        name="lookup",
    )(row_ids, table)
    dma = pltpu.SemaphoreType.DMA
    layer_out, row_grads = pl.pallas_call(
        functools.partial(layer_kernel, n, tabs),
        out_shape=(
            jax.ShapeDtypeStruct((1, count, width), bf16),
            jax.ShapeDtypeStruct((count, width), bf16),
        ),
        in_specs=[smem] * 4 + [vmem] * 4,
        out_specs=(vmem, vmem),
        scratch_shapes=[
            pltpu.VMEM((n, count, width), bf16),
            pltpu.VMEM((n, count, width), bf16),
            pltpu.VMEM((3, n, count, width), bf16),
            pltpu.VMEM((3, n, H, count // 2, count // 2), bf16),
            pltpu.VMEM((3, n, H, count // 2, count // 2), bf16),
            pltpu.VMEM((3, n, H, count // 2, count // 2), bf16),
            pltpu.VMEM((4, count, width), f32),
            pltpu.VMEM((count, width), f32),
            pltpu.VMEM((count, width), bf16),
            pltpu.VMEM((count, width), f32),
            pltpu.VMEM((count, width), f32),
            pltpu.VMEM((count, width), f32),
            pltpu.VMEM((count, width), f32),
            pltpu.VMEM((count, width), f32),
            pltpu.VMEM((count, width), f32),
            pltpu.VMEM((count, width), f32),
            pltpu.VMEM((count, 128), f32),
            pltpu.VMEM((count, 128), jnp.int32),
            pltpu.VMEM((tabs, BROWS, width), bf16),
            pltpu.VMEM((tabs, BROWS, width), bf16),
            pltpu.VMEM((tabs, BROWS, width), bf16),
            pltpu.VMEM((tabs, BROWS, width), bf16),
            dma((3, n)),
            dma((n,)),
            dma((3, n)),
            dma((n,)),
            dma((tabs,)),
            dma((tabs,)),
            dma((tabs,)),
            dma((tabs,)),
        ],
        compiler_params=pltpu.CompilerParams(
            collective_id=0, has_side_effects=True, vmem_limit_bytes=60 * 1024 * 1024
        ),
        name="layer",
    )(dests, slots, lengths, tile_mask, looked, w_in, w_out, og)
    table_grad = pl.pallas_call(
        scatter_kernel,
        out_shape=jax.ShapeDtypeStruct((1, 1, table_rows, width), bf16),
        grid=(table_rows // cut,),
        in_specs=[ids_spec, rows_spec],
        out_specs=tile_spec,
        name="table_grad",
    )(row_ids, row_grads)
    return layer_out, table_grad


def solution(mesh):
    in_specs = (
        P("ctx", "tab", None, None),
        P("ctx", "tab", None),
        P("ctx", None, None),
        P("ctx", None, None),
        P("tab", None),
        P("tab", None, None),
        P(),
        P(),
        P("tab", "ctx", None),
    )
    out_specs = (P("tab", "ctx", None), P("ctx", "tab", None, None))
    return jax.shard_map(
        functools.partial(body, mesh.shape["ctx"], mesh.shape["tab"]),
        mesh=mesh,
        in_specs=in_specs,
        out_specs=out_specs,
        check_vma=False,
    )
```

```python
import functools

import jax
import jax.numpy as jnp
from jax import lax
from jax.experimental import pallas as pl
from jax.experimental.pallas import tpu as pltpu
from jax.sharding import PartitionSpec as P

H = 4
BROWS = 64
NBLK = 4
FAST = 2

epsilon = 1e-05
MESH = pl.DeviceIdType.MESH
NT = (((1,), (1,)), ((), ()))
TN = (((0,), (0,)), ((), ()))


def dot(a, b):
    return jnp.dot(a, b, preferred_element_type=jnp.float32)


def dot_nt(a, b):
    return lax.dot_general(a, b, NT, preferred_element_type=jnp.float32)


def layer_statistics(inputs):
    row_mean = jnp.mean(inputs, axis=-1, keepdims=True)
    centred = inputs - row_mean
    inverse = lax.rsqrt(jnp.mean(centred * centred, axis=-1, keepdims=True) + epsilon)
    return (centred * inverse, inverse)


def norm_backward_pass(incoming, normalized, inverse):
    first = jnp.mean(incoming, axis=-1, keepdims=True)
    second = jnp.mean(incoming * normalized, axis=-1, keepdims=True)
    return inverse * (incoming - first - normalized * second)


def silu_half(half):
    return half * (1.0 + jnp.tanh(half))


def slope_half(half, tanh):
    return (0.5 + 0.5 * tanh) * (1.0 + half * (1.0 - tanh))


def scatter_kernel(ids_ref, grads_ref, out_ref, held, sems):
    count = ids_ref.shape[2]
    pieces = sems.shape[0]
    rows = held.shape[0] // pieces
    copies = []
    for i in range(pieces):
        row = lax.broadcasted_iota(jnp.int32, (rows, count), 0) + i * rows
        pick = jnp.where(row == ids_ref[0], 1.0, 0.0).astype(jnp.bfloat16)
        at = pl.ds(i * rows, rows)
        held[at, :] = dot(pick, grads_ref[...]).astype(held.dtype)
        copy = pltpu.make_async_copy(held.at[at], out_ref.at[0, 0, at], sems.at[i])
        copy.start()
        copies.append(copy)
    for copy in copies:
        copy.wait()


def layer_kernel(
    n,
    tabs,
    dests,
    slots,
    lengths,
    tiles,
    ids_ref,
    table_ref,
    w_in_ref,
    w_out_ref,
    og_ref,
    out_ref,
    grads_ref,
    xg,
    dg,
    vqk,
    gq,
    pk,
    gk,
    pre,
    attn,
    seq,
    dq,
    dk,
    dv,
    dup,
    dm,
    up,
    xhat,
    xinv,
    startq,
    route_out,
    route_in,
    back_out,
    back_in,
    xs,
    xr,
    ds_,
    dr,
    rs,
    rr,
    bs,
    br,
    held,
    w_in,
    w_out,
    looked,
    local_sems,
):
    me = lax.axis_index("ctx")
    tab = lax.axis_index("tab")
    levels = n // FAST
    z = me // FAST
    x = me % FAST
    rows, width = looked.shape
    half = rows // 2
    per_half = half // BROWS
    hd = width // H
    scale = hd ** (-0.5)

    pieces = local_sems.shape[0] - 2
    piece = held.shape[0] // pieces
    loads = [
        pltpu.make_async_copy(
            table_ref.at[0, 0, pl.ds(i * piece, piece)],
            held.at[pl.ds(i * piece, piece)],
            local_sems.at[i],
        )
        for i in range(pieces)
    ]
    load_out = pltpu.make_async_copy(w_out_ref, w_out, local_sems.at[pieces])
    load_in = pltpu.make_async_copy(w_in_ref, w_in, local_sems.at[pieces + 1])
    for load in loads:
        load.start()
    load_out.start()
    load_in.start()

    barrier = pltpu.get_barrier_semaphore()

    def greet_ctx(k, carry):
        pl.semaphore_signal(
            barrier, inc=1, device_id=(lax.rem(me + k, n), tab), device_id_type=MESH
        )
        return carry

    def greet_tab(k, carry):
        pl.semaphore_signal(
            barrier, inc=1, device_id=(me, lax.rem(tab + k, tabs)), device_id_type=MESH
        )
        return carry

    lax.fori_loop(1, n, greet_ctx, 0)
    lax.fori_loop(1, tabs, greet_tab, 0)

    line = jnp.broadcast_to(ids_ref[0], (rows, rows))
    at_row = lax.broadcasted_iota(jnp.int32, (rows, rows), 0)
    at_lane = lax.broadcasted_iota(jnp.int32, (rows, rows), 1)
    column = jnp.where(at_row == at_lane, line, 0).astype(jnp.float32)
    column = jnp.sum(column, axis=1, keepdims=True)
    column = jnp.broadcast_to(column, (rows, 128)).astype(jnp.int32)
    lane = lax.broadcasted_iota(jnp.int32, (rows, 128), 1)
    found = jnp.zeros((rows, width), jnp.float32)
    for i, load in enumerate(loads):
        load.wait()
        picks = [
            jnp.where(column == lane + (i * piece + k * 128), 1.0, 0.0)
            for k in range(piece // 128)
        ]
        pick = jnp.concatenate(picks, axis=1).astype(jnp.bfloat16)
        found += dot(pick, held[pl.ds(i * piece, piece), :])
    looked[...] = found.astype(jnp.bfloat16)

    def choose(hit, block, other):
        on = jnp.full(block.shape, hit.astype(jnp.int32)) > 0
        return jnp.where(on, block, other)

    def block_for(t):
        block = looked[0:BROWS, :]
        for p in range(1, NBLK):
            other = looked[p * BROWS : (p + 1) * BROWS, :]
            block = choose(dests[0, tab, p] == t, other, block)
        return block

    def route_copy(src, dst, send, recv, t):
        return pltpu.make_async_remote_copy(
            src_ref=src.at[t],
            dst_ref=dst.at[tab],
            send_sem=send.at[t],
            recv_sem=recv.at[tab],
            device_id=(me, t),
            device_id_type=MESH,
        )

    def route_wait(src, dst, send, recv, t):
        pltpu.make_async_remote_copy(
            src_ref=src.at[t],
            dst_ref=dst.at[t],
            send_sem=send.at[t],
            recv_sem=recv.at[t],
            device_id=(me, t),
            device_id_type=MESH,
        ).wait()

    for k in range(tabs):
        t = lax.rem(tab + k, tabs)
        if k == 0:
            route_in[tab] = block_for(t)
        else:
            route_out[t] = block_for(t)

    pl.semaphore_wait(barrier, n + tabs - 2)

    for k in range(1, tabs):
        route_copy(route_out, route_in, rs, rr, lax.rem(tab + k, tabs)).start()

    load_out.wait()
    dm[...] = dot_nt(og_ref[0], w_out[...])

    def starts_of(pos):
        end = jnp.int32(0)
        start = jnp.zeros_like(pos)
        for e in range(lengths.shape[1]):
            end = end + lengths[0, e]
            start = jnp.where(pos >= end, end, start)
        return start

    def base_of(s, side):
        return (2 * n - 1 - s) * half if side else s * half

    for side in range(2):
        local = lax.broadcasted_iota(jnp.int32, (half, 128), 0)
        startq[side * half : (side + 1) * half, :] = starts_of(local + base_of(me, side))
    attn[...] = jnp.zeros_like(attn)

    def tile_rows(pick):
        block = lax.broadcasted_iota(jnp.int32, (BROWS, half), 1) // BROWS
        stripes = []
        for a in range(per_half):
            line = jnp.full((BROWS, half), pick(a, 0))
            for b in range(1, per_half):
                line = jnp.where(block == b, pick(a, b), line)
            stripes.append(line)
        return jnp.concatenate(stripes, axis=0) > 0

    def query_mask(s, mine, theirs):
        at, to = base_of(me, mine), base_of(s, theirs)
        own = lax.broadcasted_iota(jnp.int32, (half, half), 0) + at
        other = lax.broadcasted_iota(jnp.int32, (half, half), 1) + to
        first = startq[mine * half : (mine + 1) * half, :]
        at, to = at // BROWS, to // BROWS
        on = tile_rows(lambda a, b: tiles[0, at + a, to + b])
        return jnp.where((other <= own) & (other >= first) & on, 1.0, 0.0)

    def key_mask(s, mine, theirs):
        at, to = base_of(me, mine), base_of(s, theirs)
        own = lax.broadcasted_iota(jnp.int32, (half, half), 0) + at
        other = lax.broadcasted_iota(jnp.int32, (half, half), 1) + to
        first = starts_of(lax.broadcasted_iota(jnp.int32, (1, half), 1) + to)
        at, to = at // BROWS, to // BROWS
        on = tile_rows(lambda a, b: tiles[0, to + b, at + a])
        return jnp.where((own <= other) & (own >= first) & on, 1.0, 0.0)

    def side_rows(side):
        return slice(side * half, (side + 1) * half)

    def take(part, s, side, h):
        return vqk[part, s, side_rows(side), h * hd : (h + 1) * hd]

    def project(s):
        block = xg[s]
        for part in range(3):
            lo = (part + 1) * width
            value = dot(block, w_in[:, lo : lo + width])
            vqk[part, s] = silu_half(0.5 * value).astype(jnp.bfloat16)

    def quads(s):
        return (
            (s <= me, 0, 0, 1, 1),
            (s >= n - 1 - me, 1, 0, 0, 1),
            (s >= me, 1, 1, 0, 0),
        )

    def forward(s):
        project(s)
        for i, (when, qm, kt, km, qt) in enumerate(quads(s)):

            @pl.when(when)
            def _(i=i, qm=qm, kt=kt, km=km, qt=qt):
                mask = query_mask(s, qm, kt)
                scaled = mask * scale
                mask_k = key_mask(s, km, qt)
                scaled_k = mask_k * scale
                for h in range(H):
                    cut = slice(h * hd, (h + 1) * hd)
                    halfs = dot_nt(take(1, me, qm, h), take(2, s, kt, h)) * (0.5 * scale)
                    tanh = jnp.tanh(halfs)
                    probs = (halfs * (1.0 + tanh) * mask).astype(jnp.bfloat16)
                    gq[i, s, h] = (slope_half(halfs, tanh) * scaled).astype(jnp.bfloat16)
                    attn[side_rows(qm), cut] += dot(probs, take(0, s, kt, h))
                    halfs = dot_nt(take(2, me, km, h), take(1, s, qt, h)) * (0.5 * scale)
                    tanh = jnp.tanh(halfs)
                    pk[i, s, h] = (halfs * (1.0 + tanh) * mask_k).astype(jnp.bfloat16)
                    gk[i, s, h] = (slope_half(halfs, tanh) * scaled_k).astype(jnp.bfloat16)

    def query_back(s):
        for i, (when, qm, kt, _, _) in enumerate(quads(s)):

            @pl.when(when)
            def _(i=i, qm=qm, kt=kt):
                for h in range(H):
                    cut = slice(h * hd, (h + 1) * hd)
                    slope = gq[i, s, h].astype(jnp.float32)
                    dsc = dot_nt(dg[me, side_rows(qm), cut], take(0, s, kt, h)) * slope
                    dq[side_rows(qm), cut] += dot(
                        dsc.astype(jnp.bfloat16), take(2, s, kt, h)
                    )

    def key_back(s):
        for i, (when, _, _, km, qt) in enumerate(quads(s)):

            @pl.when(when)
            def _(i=i, km=km, qt=qt):
                for h in range(H):
                    cut = slice(h * hd, (h + 1) * hd)
                    grad = dg[s, side_rows(qt), cut]
                    slope = gk[i, s, h].astype(jnp.float32)
                    dsc = dot_nt(take(0, me, km, h), grad) * slope
                    dk[side_rows(km), cut] += dot(
                        dsc.astype(jnp.bfloat16), take(1, s, qt, h)
                    )
                    dv[side_rows(km), cut] += dot(pk[i, s, h], grad)

    def gather(buf, send, recv, wanted, needed, compute, filler):
        partner = z * FAST + (FAST - 1 - x)

        def copy(s, side, way):
            to = (me - FAST, me + FAST, partner)[way]
            at = pl.ds(side * half, half)
            return pltpu.make_async_remote_copy(
                src_ref=buf.at[s, at],
                dst_ref=buf.at[s, at],
                send_sem=send.at[way, side, s],
                recv_sem=recv.at[side, s],
                device_id=(to, tab),
                device_id_type=MESH,
            )

        def ways(zz, side, action):
            s = zz * FAST + x

            @pl.when((zz >= z) & (z > 0) & wanted(0, s, side, z))
            def _():
                action(copy(s, side, 0))

            @pl.when((zz <= z) & (z < levels - 1) & wanted(1, s, side, z))
            def _():
                action(copy(s, side, 1))

            @pl.when(needed(partner, s, side))
            def _():
                action(copy(s, side, 2))

        def level(k, i):
            zz = z + jnp.where(i == 0, -k, k)
            there = (k >= 0) & (k < levels) & (zz >= 0) & (zz < levels)
            return zz, there & ((k > 0) | (i == 0))

        def step(k, carry):
            for i in range(2):
                zz, there = level(k, i)

                @pl.when(there)
                def _(i=i, zz=zz):
                    s = zz * FAST + x
                    for side in range(2):
                        got = wanted(1, s, side, z - 1) if i == 0 else wanted(0, s, side, z + 1)

                        @pl.when((k > 0) & got)
                        def _(side=side):
                            copy(s, side, 2).wait_recv()

                        ways(zz, side, lambda c: c.start())

            filler(k)

            def own_column(i, carry):
                zz, there = level(k, i)

                @pl.when(there)
                def _():
                    compute(zz * FAST + x)

                return carry

            def other_column(i, carry):
                zz, there = level(k - 1, i)

                @pl.when(there)
                def _():
                    s = zz * FAST + (FAST - 1 - x)
                    for side in range(2):

                        @pl.when(needed(me, s, side))
                        def _(side=side):
                            copy(s, side, 2).wait_recv()

                    compute(s)

                return carry

            lax.fori_loop(0, 2, own_column, 0)
            lax.fori_loop(0, 2, other_column, 0)
            return carry

        lax.fori_loop(0, levels + 1, step, 0)

        def drain(zz, carry):
            for side in range(2):
                ways(zz, side, lambda c: c.wait_send())
            return carry

        lax.fori_loop(0, levels, drain, 0)

    load_in.wait()
    for k in range(1, tabs):
        route_wait(route_out, route_in, rs, rr, lax.rem(tab + k, tabs))

    def arrives(s, t):
        count = jnp.int32(0)
        for p in range(NBLK):
            hit = (dests[0, t, p] == tab) & (slots[0, t, p] == s)
            count += hit.astype(jnp.int32)
        return count > 0

    for s in range(NBLK):
        block = route_in[0]
        for t in range(1, tabs):
            block = choose(arrives(s, t), route_in[t], block)
        seq[s * BROWS : (s + 1) * BROWS, :] = block

    normal, inverse = layer_statistics(seq[...].astype(jnp.float32))
    xg[me] = normal.astype(jnp.bfloat16)
    xhat[...] = normal
    xinv[...] = jnp.broadcast_to(inverse, xinv.shape)

    def part_of(part):
        return w_in[:, part * width : (part + 1) * width]

    def own_rows(j):
        @pl.when(j == 0)
        def _():
            for part in range(4):
                halfs = 0.5 * dot(xg[me], part_of(part))
                tanh = jnp.tanh(halfs)
                pre[part] = slope_half(halfs, tanh)
                if part == 0:
                    act = (halfs * (1.0 + tanh)).astype(jnp.bfloat16)
                    up[...] = act.astype(jnp.float32)

    def always(*_):
        return me >= 0

    gather(xg, xs, xr, always, always, forward, own_rows)

    attn_hat, attn_inverse = layer_statistics(attn[...])
    dg[me] = norm_backward_pass(dm[...] * up[...], attn_hat, attn_inverse).astype(
        jnp.bfloat16
    )
    attn[...] = attn_hat
    dq[...] = jnp.zeros_like(dq)
    dk[...] = jnp.zeros_like(dk)
    dv[...] = jnp.zeros_like(dv)

    def d_pre(part, grad):
        return dot_nt((grad * pre[part]).astype(jnp.bfloat16), part_of(part))

    def own_back(j):
        @pl.when(j == 0)
        def _():
            attn_hat = attn[...]
            mixed = (attn_hat * up[...]).astype(jnp.bfloat16)
            out_ref[0] = (seq[...].astype(jnp.float32) + dot(mixed, w_out[...])).astype(
                jnp.bfloat16
            )
            dup[...] = d_pre(0, dm[...] * attn_hat)

        @pl.when(j < levels)
        def _():
            def one(i, carry):
                query_back(j * FAST + i)
                return carry

            lax.fori_loop(0, FAST, one, 0)

        @pl.when(j == levels)
        def _():
            dup[...] += d_pre(2, dq[...])

    def needed(d, s, side):
        if side == 0:
            return d <= s
        return (s <= d) | (s >= n - 1 - d)

    def wanted(way, s, side, at):
        if side == 0:
            return me >= 0 if way == 0 else me < 0
        return n - 1 - s <= at * FAST - 1 if way == 0 else me >= 0

    gather(dg, ds_, dr, wanted, needed, key_back, own_back)

    normalized = dup[...] + d_pre(1, dv[...]) + d_pre(3, dk[...])
    attn[...] = og_ref[0].astype(jnp.float32) + norm_backward_pass(
        normalized, xhat[...], xinv[:, 0:1]
    )

    def back_block(t):
        block = attn[0:BROWS, :]
        for s in range(1, NBLK):
            other = attn[s * BROWS : (s + 1) * BROWS, :]
            block = choose(arrives(s, t), other, block)
        return block.astype(jnp.bfloat16)

    for k in range(tabs):
        t = lax.rem(tab + k, tabs)
        if k == 0:
            back_in[tab] = back_block(t)
        else:
            back_out[t] = back_block(t)
            route_copy(back_out, back_in, bs, br, t).start()
    for k in range(1, tabs):
        route_wait(back_out, back_in, bs, br, lax.rem(tab + k, tabs))
    for p in range(NBLK):
        block = back_in[0]
        for t in range(1, tabs):
            block = choose(dests[0, tab, p] == t, back_in[t], block)
        grads_ref[p * BROWS : (p + 1) * BROWS, :] = block


def body(n, tabs, table, row_ids, dests, slots, lengths, tile_mask, w_in, w_out, og):
    count = row_ids.shape[2]
    width = w_out.shape[0]
    table_rows = table.shape[2]
    pieces = 8
    bf16, f32 = jnp.bfloat16, jnp.float32
    vmem = pl.BlockSpec(memory_space=pltpu.VMEM)
    smem = pl.BlockSpec(memory_space=pltpu.SMEM)
    hbm = pl.BlockSpec(memory_space=pl.ANY)
    dma = pltpu.SemaphoreType.DMA
    layer_out, row_grads = pl.pallas_call(
        functools.partial(layer_kernel, n, tabs),
        out_shape=(
            jax.ShapeDtypeStruct((1, count, width), bf16),
            jax.ShapeDtypeStruct((count, width), bf16),
        ),
        in_specs=[smem] * 4 + [vmem, hbm, hbm, hbm, vmem],
        out_specs=(vmem, vmem),
        scratch_shapes=[
            pltpu.VMEM((n, count, width), bf16),
            pltpu.VMEM((n, count, width), bf16),
            pltpu.VMEM((3, n, count, width), bf16),
            pltpu.VMEM((3, n, H, count // 2, count // 2), bf16),
            pltpu.VMEM((3, n, H, count // 2, count // 2), bf16),
            pltpu.VMEM((3, n, H, count // 2, count // 2), bf16),
            pltpu.VMEM((4, count, width), f32),
            pltpu.VMEM((count, width), f32),
            pltpu.VMEM((count, width), bf16),
            pltpu.VMEM((count, width), f32),
            pltpu.VMEM((count, width), f32),
            pltpu.VMEM((count, width), f32),
            pltpu.VMEM((count, width), f32),
            pltpu.VMEM((count, width), f32),
            pltpu.VMEM((count, width), f32),
            pltpu.VMEM((count, width), f32),
            pltpu.VMEM((count, 128), f32),
            pltpu.VMEM((count, 128), jnp.int32),
            pltpu.VMEM((tabs, BROWS, width), bf16),
            pltpu.VMEM((tabs, BROWS, width), bf16),
            pltpu.VMEM((tabs, BROWS, width), bf16),
            pltpu.VMEM((tabs, BROWS, width), bf16),
            dma((3, 2, n)),
            dma((2, n)),
            dma((3, 2, n)),
            dma((2, n)),
            dma((tabs,)),
            dma((tabs,)),
            dma((tabs,)),
            dma((tabs,)),
            pltpu.VMEM((table_rows, width), bf16),
            pltpu.VMEM(w_in.shape, bf16),
            pltpu.VMEM(w_out.shape, bf16),
            pltpu.VMEM((count, width), bf16),
            dma((pieces + 2,)),
        ],
        compiler_params=pltpu.CompilerParams(
            collective_id=0, has_side_effects=True, vmem_limit_bytes=60 * 1024 * 1024
        ),
        name="layer",
    )(dests, slots, lengths, tile_mask, row_ids, table, w_in, w_out, og)
    table_grad = pl.pallas_call(
        scatter_kernel,
        out_shape=jax.ShapeDtypeStruct((1, 1, table_rows, width), bf16),
        in_specs=[vmem, vmem],
        out_specs=hbm,
        scratch_shapes=[pltpu.VMEM((table_rows, width), bf16), dma((pieces,))],
        name="table_grad",
    )(row_ids, row_grads)
    return layer_out, table_grad


def solution(mesh):
    in_specs = (
        P("ctx", "tab", None, None),
        P("ctx", "tab", None),
        P("ctx", None, None),
        P("ctx", None, None),
        P("tab", None),
        P("tab", None, None),
        P(),
        P(),
        P("tab", "ctx", None),
    )
    out_specs = (P("tab", "ctx", None), P("ctx", "tab", None, None))
    return jax.shard_map(
        functools.partial(body, mesh.shape["ctx"], mesh.shape["tab"]),
        mesh=mesh,
        in_specs=in_specs,
        out_specs=out_specs,
        check_vma=False,
    )
```

```python
import functools

import jax
import jax.numpy as jnp
from jax import lax
from jax.experimental import pallas as pl
from jax.experimental.pallas import tpu as pltpu
from jax.sharding import PartitionSpec as P

H = 4
BROWS = 64
NBLK = 4
FAST = 2
ALONG = 1

epsilon = 1e-05
MESH = pl.DeviceIdType.MESH
NT = (((1,), (1,)), ((), ()))
TN = (((0,), (0,)), ((), ()))


def dot(a, b):
    return jnp.dot(a, b, preferred_element_type=jnp.float32)


def dot_nt(a, b):
    return lax.dot_general(a, b, NT, preferred_element_type=jnp.float32)


def layer_statistics(inputs):
    row_mean = jnp.mean(inputs, axis=-1, keepdims=True)
    centred = inputs - row_mean
    inverse = lax.rsqrt(jnp.mean(centred * centred, axis=-1, keepdims=True) + epsilon)
    return (centred * inverse, inverse)


def norm_backward_pass(incoming, normalized, inverse):
    first = jnp.mean(incoming, axis=-1, keepdims=True)
    second = jnp.mean(incoming * normalized, axis=-1, keepdims=True)
    return inverse * (incoming - first - normalized * second)


def silu_half(half):
    return half * (1.0 + jnp.tanh(half))


def slope_half(half, tanh):
    return (0.5 + 0.5 * tanh) * (1.0 + half * (1.0 - tanh))


def scatter_kernel(ids_ref, grads_ref, layer_ref, out_ref, layer_out_ref, held, sems):
    count = ids_ref.shape[2]
    pieces = sems.shape[0] - 1
    layer = pltpu.make_async_copy(layer_ref, layer_out_ref, sems.at[pieces])
    layer.start()
    rows = held.shape[0] // pieces
    copies = []
    for i in range(pieces):
        row = lax.broadcasted_iota(jnp.int32, (rows, count), 0) + i * rows
        pick = jnp.where(row == ids_ref[0], 1.0, 0.0).astype(jnp.bfloat16)
        at = pl.ds(i * rows, rows)
        held[at, :] = dot(pick, grads_ref[...]).astype(held.dtype)
        copy = pltpu.make_async_copy(held.at[at], out_ref.at[0, 0, at], sems.at[i])
        copy.start()
        copies.append(copy)
    for copy in copies:
        copy.wait()
    layer.wait()


def layer_kernel(
    n,
    tabs,
    dests,
    slots,
    lengths,
    tiles,
    ids_ref,
    table_ref,
    w_in_ref,
    w_out_ref,
    og_in_ref,
    out_ref,
    grads_ref,
    xg,
    dg,
    vqk,
    gq,
    pk,
    gk,
    pre,
    attn,
    seq,
    dq,
    dk,
    dv,
    dup,
    dm,
    up,
    xhat,
    xinv,
    startq,
    route_out,
    route_in,
    back_out,
    back_in,
    xs,
    xr,
    ds_,
    dr,
    rs,
    rr,
    bs,
    br,
    held,
    w_in,
    w_out,
    looked,
    og_ref,
    local_sems,
):
    me = lax.axis_index("ctx")
    tab = lax.axis_index("tab")
    levels = n // FAST
    z = me // FAST
    x = me % FAST
    rows, width = looked.shape
    half = rows // 2
    per_half = half // BROWS
    hd = width // H
    scale = hd ** (-0.5)

    pieces = local_sems.shape[0] - 3
    piece = held.shape[0] // pieces
    loads = [
        pltpu.make_async_copy(
            table_ref.at[0, 0, pl.ds(i * piece, piece)],
            held.at[pl.ds(i * piece, piece)],
            local_sems.at[i],
        )
        for i in range(pieces)
    ]
    load_out = pltpu.make_async_copy(w_out_ref, w_out, local_sems.at[pieces])
    load_in = pltpu.make_async_copy(w_in_ref, w_in, local_sems.at[pieces + 1])
    for load in loads:
        load.start()
    load_out.start()
    load_og = pltpu.make_async_copy(og_in_ref, og_ref, local_sems.at[pieces + 2])
    load_og.start()
    load_in.start()

    barrier = pltpu.get_barrier_semaphore()

    def greet_ctx(k, carry):
        pl.semaphore_signal(
            barrier, inc=1, device_id=(lax.rem(me + k, n), tab), device_id_type=MESH
        )
        return carry

    def greet_tab(k, carry):
        pl.semaphore_signal(
            barrier, inc=1, device_id=(me, lax.rem(tab + k, tabs)), device_id_type=MESH
        )
        return carry

    lax.fori_loop(1, n, greet_ctx, 0)
    lax.fori_loop(1, tabs, greet_tab, 0)

    line = jnp.broadcast_to(ids_ref[0], (rows, rows))
    at_row = lax.broadcasted_iota(jnp.int32, (rows, rows), 0)
    at_lane = lax.broadcasted_iota(jnp.int32, (rows, rows), 1)
    column = jnp.where(at_row == at_lane, line, 0).astype(jnp.float32)
    column = jnp.sum(column, axis=1, keepdims=True)
    column = jnp.broadcast_to(column, (rows, 128)).astype(jnp.int32)
    lane = lax.broadcasted_iota(jnp.int32, (rows, 128), 1)
    found = jnp.zeros((rows, width), jnp.float32)
    for i, load in enumerate(loads):
        load.wait()
        picks = [
            jnp.where(column == lane + (i * piece + k * 128), 1.0, 0.0)
            for k in range(piece // 128)
        ]
        pick = jnp.concatenate(picks, axis=1).astype(jnp.bfloat16)
        found += dot(pick, held[pl.ds(i * piece, piece), :])
    looked[...] = found.astype(jnp.bfloat16)

    def choose(hit, block, other):
        on = jnp.full(block.shape, hit.astype(jnp.int32)) > 0
        return jnp.where(on, block, other)

    def block_for(t):
        block = looked[0:BROWS, :]
        for p in range(1, NBLK):
            other = looked[p * BROWS : (p + 1) * BROWS, :]
            block = choose(dests[0, tab, p] == t, other, block)
        return block

    def route_copy(src, dst, send, recv, t):
        return pltpu.make_async_remote_copy(
            src_ref=src.at[t],
            dst_ref=dst.at[tab],
            send_sem=send.at[t],
            recv_sem=recv.at[tab],
            device_id=(me, t),
            device_id_type=MESH,
        )

    def route_wait(src, dst, send, recv, t):
        pltpu.make_async_remote_copy(
            src_ref=src.at[t],
            dst_ref=dst.at[t],
            send_sem=send.at[t],
            recv_sem=recv.at[t],
            device_id=(me, t),
            device_id_type=MESH,
        ).wait()

    for k in range(tabs):
        t = lax.rem(tab + k, tabs)
        if k == 0:
            route_in[tab] = block_for(t)
        else:
            route_out[t] = block_for(t)

    pl.semaphore_wait(barrier, n + tabs - 2)

    for k in range(1, tabs):
        route_copy(route_out, route_in, rs, rr, lax.rem(tab + k, tabs)).start()

    load_out.wait()
    load_og.wait()
    dm[...] = dot_nt(og_ref[0], w_out[...])

    def starts_of(pos):
        end = jnp.int32(0)
        start = jnp.zeros_like(pos)
        for e in range(lengths.shape[1]):
            end = end + lengths[0, e]
            start = jnp.where(pos >= end, end, start)
        return start

    def base_of(s, side):
        return (2 * n - 1 - s) * half if side else s * half

    for side in range(2):
        local = lax.broadcasted_iota(jnp.int32, (half, 128), 0)
        startq[side * half : (side + 1) * half, :] = starts_of(local + base_of(me, side))
    attn[...] = jnp.zeros_like(attn)

    def tile_rows(pick):
        block = lax.broadcasted_iota(jnp.int32, (BROWS, half), 1) // BROWS
        stripes = []
        for a in range(per_half):
            line = jnp.full((BROWS, half), pick(a, 0))
            for b in range(1, per_half):
                line = jnp.where(block == b, pick(a, b), line)
            stripes.append(line)
        return jnp.concatenate(stripes, axis=0) > 0

    def query_mask(s, mine, theirs):
        at, to = base_of(me, mine), base_of(s, theirs)
        own = lax.broadcasted_iota(jnp.int32, (half, half), 0) + at
        other = lax.broadcasted_iota(jnp.int32, (half, half), 1) + to
        first = startq[mine * half : (mine + 1) * half, :]
        at, to = at // BROWS, to // BROWS
        on = tile_rows(lambda a, b: tiles[0, at + a, to + b])
        return jnp.where((other <= own) & (other >= first) & on, 1.0, 0.0)

    def key_mask(s, mine, theirs):
        at, to = base_of(me, mine), base_of(s, theirs)
        own = lax.broadcasted_iota(jnp.int32, (half, half), 0) + at
        other = lax.broadcasted_iota(jnp.int32, (half, half), 1) + to
        first = starts_of(lax.broadcasted_iota(jnp.int32, (1, half), 1) + to)
        at, to = at // BROWS, to // BROWS
        on = tile_rows(lambda a, b: tiles[0, to + b, at + a])
        return jnp.where((own <= other) & (own >= first) & on, 1.0, 0.0)

    def side_rows(side):
        return slice(side * half, (side + 1) * half)

    def take(part, s, side, h):
        return vqk[part, s, side_rows(side), h * hd : (h + 1) * hd]

    def project(s):
        block = xg[s]
        for part in range(3):
            lo = (part + 1) * width
            value = dot(block, w_in[:, lo : lo + width])
            vqk[part, s] = silu_half(0.5 * value).astype(jnp.bfloat16)

    def quads(s):
        return (
            (s <= me, 0, 0, 1, 1),
            (s >= n - 1 - me, 1, 0, 0, 1),
            (s >= me, 1, 1, 0, 0),
        )

    def forward(s):
        project(s)
        for i, (when, qm, kt, km, qt) in enumerate(quads(s)):

            @pl.when(when)
            def _(i=i, qm=qm, kt=kt, km=km, qt=qt):
                mask = query_mask(s, qm, kt)
                scaled = mask * scale
                mask_k = key_mask(s, km, qt)
                scaled_k = mask_k * scale
                for h in range(H):
                    cut = slice(h * hd, (h + 1) * hd)
                    halfs = dot_nt(take(1, me, qm, h), take(2, s, kt, h)) * (0.5 * scale)
                    tanh = jnp.tanh(halfs)
                    probs = (halfs * (1.0 + tanh) * mask).astype(jnp.bfloat16)
                    gq[i, s, h] = (slope_half(halfs, tanh) * scaled).astype(jnp.bfloat16)
                    attn[side_rows(qm), cut] += dot(probs, take(0, s, kt, h))
                    halfs = dot_nt(take(2, me, km, h), take(1, s, qt, h)) * (0.5 * scale)
                    tanh = jnp.tanh(halfs)
                    pk[i, s, h] = (halfs * (1.0 + tanh) * mask_k).astype(jnp.bfloat16)
                    gk[i, s, h] = (slope_half(halfs, tanh) * scaled_k).astype(jnp.bfloat16)

    def query_back(s):
        for i, (when, qm, kt, _, _) in enumerate(quads(s)):

            @pl.when(when)
            def _(i=i, qm=qm, kt=kt):
                for h in range(H):
                    cut = slice(h * hd, (h + 1) * hd)
                    slope = gq[i, s, h].astype(jnp.float32)
                    dsc = dot_nt(dg[me, side_rows(qm), cut], take(0, s, kt, h)) * slope
                    dq[side_rows(qm), cut] += dot(
                        dsc.astype(jnp.bfloat16), take(2, s, kt, h)
                    )

    def key_back(s):
        for i, (when, _, _, km, qt) in enumerate(quads(s)):

            @pl.when(when)
            def _(i=i, km=km, qt=qt):
                for h in range(H):
                    cut = slice(h * hd, (h + 1) * hd)
                    grad = dg[s, side_rows(qt), cut]
                    slope = gk[i, s, h].astype(jnp.float32)
                    dsc = dot_nt(take(0, me, km, h), grad) * slope
                    dk[side_rows(km), cut] += dot(
                        dsc.astype(jnp.bfloat16), take(1, s, qt, h)
                    )
                    dv[side_rows(km), cut] += dot(pk[i, s, h], grad)

    def gather(buf, send, recv, wanted, needed, compute, filler):
        partner = z * FAST + (FAST - 1 - x)

        def copy(s, side, way):
            to = (me - FAST, me + FAST, partner)[way]
            at = pl.ds(side * half, half)
            return pltpu.make_async_remote_copy(
                src_ref=buf.at[s, at],
                dst_ref=buf.at[s, at],
                send_sem=send.at[way, side, s],
                recv_sem=recv.at[side, s],
                device_id=(to, tab),
                device_id_type=MESH,
            )

        def ways(zz, side, action):
            s = zz * FAST + x

            @pl.when((zz >= z) & (z > 0) & wanted(0, s, side, z))
            def _():
                action(copy(s, side, 0))

            @pl.when((zz <= z) & (z < levels - 1) & wanted(1, s, side, z))
            def _():
                action(copy(s, side, 1))

            if side == ALONG:
                beside = (zz == z - 1) | (zz == z + 1)
                has = needed(zz * FAST + (FAST - 1 - x), s, side)
                across = needed(partner, s, side) & ~(beside & has)
            else:
                across = needed(partner, s, side)

            @pl.when(across)
            def _():
                action(copy(s, side, 2))

        def along(action):
            has = needed(me, partner, ALONG)

            @pl.when(has & (z > 0) & needed(me - FAST, partner, ALONG))
            def _():
                action(copy(partner, ALONG, 0))

            @pl.when(has & (z < levels - 1) & needed(me + FAST, partner, ALONG))
            def _():
                action(copy(partner, ALONG, 1))

        def level(k, i):
            zz = z + jnp.where(i == 0, -k, k)
            there = (k >= 0) & (k < levels) & (zz >= 0) & (zz < levels)
            return zz, there & ((k > 0) | (i == 0))

        def step(k, carry):
            for i in range(2):
                zz, there = level(k, i)

                @pl.when(there)
                def _(i=i, zz=zz):
                    s = zz * FAST + x
                    for side in range(2):
                        got = wanted(1, s, side, z - 1) if i == 0 else wanted(0, s, side, z + 1)

                        @pl.when((k > 0) & got)
                        def _(side=side):
                            copy(s, side, 2).wait_recv()

                        ways(zz, side, lambda c: c.start())

            @pl.when(k == 2)
            def _():
                along(lambda c: c.start())

            filler(k)

            def own_column(i, carry):
                zz, there = level(k, i)

                @pl.when(there)
                def _():
                    compute(zz * FAST + x)

                return carry

            def other_column(i, carry):
                last = k == levels + 1
                zz, there = level(jnp.where(last, 1, k - 1), i)

                @pl.when(there & ((k != 2) | last))
                def _():
                    s = zz * FAST + (FAST - 1 - x)
                    for side in range(2):

                        @pl.when(needed(me, s, side))
                        def _(side=side):
                            copy(s, side, 2).wait_recv()

                    compute(s)

                return carry

            lax.fori_loop(0, 2, own_column, 0)
            lax.fori_loop(0, 2, other_column, 0)
            return carry

        lax.fori_loop(0, levels + 2, step, 0)

        def drain(zz, carry):
            for side in range(2):
                ways(zz, side, lambda c: c.wait_send())
            return carry

        lax.fori_loop(0, levels, drain, 0)
        along(lambda c: c.wait_send())

    load_in.wait()
    for k in range(1, tabs):
        route_wait(route_out, route_in, rs, rr, lax.rem(tab + k, tabs))

    def arrives(s, t):
        count = jnp.int32(0)
        for p in range(NBLK):
            hit = (dests[0, t, p] == tab) & (slots[0, t, p] == s)
            count += hit.astype(jnp.int32)
        return count > 0

    for s in range(NBLK):
        block = route_in[0]
        for t in range(1, tabs):
            block = choose(arrives(s, t), route_in[t], block)
        seq[s * BROWS : (s + 1) * BROWS, :] = block

    normal, inverse = layer_statistics(seq[...].astype(jnp.float32))
    xg[me] = normal.astype(jnp.bfloat16)
    xhat[...] = normal
    xinv[...] = jnp.broadcast_to(inverse, xinv.shape)

    def part_of(part):
        return w_in[:, part * width : (part + 1) * width]

    def own_rows(j):
        @pl.when(j == 0)
        def _():
            for part in range(4):
                halfs = 0.5 * dot(xg[me], part_of(part))
                tanh = jnp.tanh(halfs)
                pre[part] = slope_half(halfs, tanh)
                if part == 0:
                    act = (halfs * (1.0 + tanh)).astype(jnp.bfloat16)
                    up[...] = act.astype(jnp.float32)

    def always(*_):
        return me >= 0

    gather(xg, xs, xr, always, always, forward, own_rows)

    attn_hat, attn_inverse = layer_statistics(attn[...])
    dg[me] = norm_backward_pass(dm[...] * up[...], attn_hat, attn_inverse).astype(
        jnp.bfloat16
    )
    attn[...] = attn_hat
    dq[...] = jnp.zeros_like(dq)
    dk[...] = jnp.zeros_like(dk)
    dv[...] = jnp.zeros_like(dv)

    def d_pre(part, grad):
        return dot_nt((grad * pre[part]).astype(jnp.bfloat16), part_of(part))

    def own_back(j):
        @pl.when(j == 0)
        def _():
            attn_hat = attn[...]
            mixed = (attn_hat * up[...]).astype(jnp.bfloat16)
            out_ref[0] = (seq[...].astype(jnp.float32) + dot(mixed, w_out[...])).astype(
                jnp.bfloat16
            )
            dup[...] = d_pre(0, dm[...] * attn_hat)

        @pl.when(j < levels)
        def _():
            def one(i, carry):
                query_back(j * FAST + i)
                return carry

            lax.fori_loop(0, FAST, one, 0)

        @pl.when(j == levels)
        def _():
            dup[...] += d_pre(2, dq[...])

    def needed(d, s, side):
        if side == 0:
            return d <= s
        return (s <= d) | (s >= n - 1 - d)

    def wanted(way, s, side, at):
        if side == 0:
            return me >= 0 if way == 0 else me < 0
        return n - 1 - s <= at * FAST - 1 if way == 0 else me >= 0

    gather(dg, ds_, dr, wanted, needed, key_back, own_back)

    normalized = dup[...] + d_pre(1, dv[...]) + d_pre(3, dk[...])
    attn[...] = og_ref[0].astype(jnp.float32) + norm_backward_pass(
        normalized, xhat[...], xinv[:, 0:1]
    )

    def back_block(t):
        block = attn[0:BROWS, :]
        for s in range(1, NBLK):
            other = attn[s * BROWS : (s + 1) * BROWS, :]
            block = choose(arrives(s, t), other, block)
        return block.astype(jnp.bfloat16)

    for k in range(tabs):
        t = lax.rem(tab + k, tabs)
        if k == 0:
            back_in[tab] = back_block(t)
        else:
            back_out[t] = back_block(t)
            route_copy(back_out, back_in, bs, br, t).start()
    for k in range(1, tabs):
        route_wait(back_out, back_in, bs, br, lax.rem(tab + k, tabs))
    for p in range(NBLK):
        block = back_in[0]
        for t in range(1, tabs):
            block = choose(dests[0, tab, p] == t, back_in[t], block)
        grads_ref[p * BROWS : (p + 1) * BROWS, :] = block


def body(n, tabs, table, row_ids, dests, slots, lengths, tile_mask, w_in, w_out, og):
    count = row_ids.shape[2]
    width = w_out.shape[0]
    table_rows = table.shape[2]
    pieces = 8
    bf16, f32 = jnp.bfloat16, jnp.float32
    vmem = pl.BlockSpec(memory_space=pltpu.VMEM)
    smem = pl.BlockSpec(memory_space=pltpu.SMEM)
    hbm = pl.BlockSpec(memory_space=pl.ANY)
    dma = pltpu.SemaphoreType.DMA
    layer_out, row_grads = pl.pallas_call(
        functools.partial(layer_kernel, n, tabs),
        out_shape=(
            jax.ShapeDtypeStruct((1, count, width), bf16),
            jax.ShapeDtypeStruct((count, width), bf16),
        ),
        in_specs=[smem] * 4 + [vmem, hbm, hbm, hbm, hbm],
        out_specs=(vmem, vmem),
        scratch_shapes=[
            pltpu.VMEM((n, count, width), bf16),
            pltpu.VMEM((n, count, width), bf16),
            pltpu.VMEM((3, n, count, width), bf16),
            pltpu.VMEM((3, n, H, count // 2, count // 2), bf16),
            pltpu.VMEM((3, n, H, count // 2, count // 2), bf16),
            pltpu.VMEM((3, n, H, count // 2, count // 2), bf16),
            pltpu.VMEM((4, count, width), f32),
            pltpu.VMEM((count, width), f32),
            pltpu.VMEM((count, width), bf16),
            pltpu.VMEM((count, width), f32),
            pltpu.VMEM((count, width), f32),
            pltpu.VMEM((count, width), f32),
            pltpu.VMEM((count, width), f32),
            pltpu.VMEM((count, width), f32),
            pltpu.VMEM((count, width), f32),
            pltpu.VMEM((count, width), f32),
            pltpu.VMEM((count, 128), f32),
            pltpu.VMEM((count, 128), jnp.int32),
            pltpu.VMEM((tabs, BROWS, width), bf16),
            pltpu.VMEM((tabs, BROWS, width), bf16),
            pltpu.VMEM((tabs, BROWS, width), bf16),
            pltpu.VMEM((tabs, BROWS, width), bf16),
            dma((3, 2, n)),
            dma((2, n)),
            dma((3, 2, n)),
            dma((2, n)),
            dma((tabs,)),
            dma((tabs,)),
            dma((tabs,)),
            dma((tabs,)),
            pltpu.VMEM((table_rows, width), bf16),
            pltpu.VMEM(w_in.shape, bf16),
            pltpu.VMEM(w_out.shape, bf16),
            pltpu.VMEM((count, width), bf16),
            pltpu.VMEM(og.shape, bf16),
            dma((pieces + 3,)),
        ],
        compiler_params=pltpu.CompilerParams(
            collective_id=0, has_side_effects=True, vmem_limit_bytes=60 * 1024 * 1024
        ),
        name="layer",
    )(dests, slots, lengths, tile_mask, row_ids, table, w_in, w_out, og)
    table_grad, layer_out = pl.pallas_call(
        scatter_kernel,
        out_shape=(
            jax.ShapeDtypeStruct((1, 1, table_rows, width), bf16),
            jax.ShapeDtypeStruct((1, count, width), bf16),
        ),
        in_specs=[vmem, vmem, vmem],
        out_specs=(hbm, hbm),
        scratch_shapes=[pltpu.VMEM((table_rows, width), bf16), dma((pieces + 1,))],
        name="table_grad",
    )(row_ids, row_grads, layer_out)
    return layer_out, table_grad


def solution(mesh):
    in_specs = (
        P("ctx", "tab", None, None),
        P("ctx", "tab", None),
        P("ctx", None, None),
        P("ctx", None, None),
        P("tab", None),
        P("tab", None, None),
        P(),
        P(),
        P("tab", "ctx", None),
    )
    out_specs = (P("tab", "ctx", None), P("ctx", "tab", None, None))
    return jax.shard_map(
        functools.partial(body, mesh.shape["ctx"], mesh.shape["tab"]),
        mesh=mesh,
        in_specs=in_specs,
        out_specs=out_specs,
        check_vma=False,
    )
```

```python
import functools

import jax
import jax.numpy as jnp
from jax import lax
from jax.experimental import pallas as pl
from jax.experimental.pallas import tpu as pltpu
from jax.sharding import PartitionSpec as P

H = 4
BROWS = 64
NBLK = 4
FAST = 2

epsilon = 1e-05
MESH = pl.DeviceIdType.MESH
NT = (((1,), (1,)), ((), ()))
TN = (((0,), (0,)), ((), ()))


def dot(a, b):
    return jnp.dot(a, b, preferred_element_type=jnp.float32)


def dot_nt(a, b):
    return lax.dot_general(a, b, NT, preferred_element_type=jnp.float32)


def layer_statistics(inputs):
    row_mean = jnp.mean(inputs, axis=-1, keepdims=True)
    centred = inputs - row_mean
    inverse = lax.rsqrt(jnp.mean(centred * centred, axis=-1, keepdims=True) + epsilon)
    return (centred * inverse, inverse)


def norm_backward_pass(incoming, normalized, inverse):
    first = jnp.mean(incoming, axis=-1, keepdims=True)
    second = jnp.mean(incoming * normalized, axis=-1, keepdims=True)
    return inverse * (incoming - first - normalized * second)


def silu_half(half):
    return half * (1.0 + jnp.tanh(half))


def slope_half(half, tanh):
    return (0.5 + 0.5 * tanh) * (1.0 + half * (1.0 - tanh))


def scatter_kernel(ids_ref, grads_ref, layer_ref, out_ref, layer_out_ref, held, sems):
    count = ids_ref.shape[2]
    pieces = sems.shape[0] - 1
    layer = pltpu.make_async_copy(layer_ref, layer_out_ref, sems.at[pieces])
    layer.start()
    rows = held.shape[0] // pieces
    copies = []
    for i in range(pieces):
        row = lax.broadcasted_iota(jnp.int32, (rows, count), 0) + i * rows
        pick = jnp.where(row == ids_ref[0], 1.0, 0.0).astype(jnp.bfloat16)
        at = pl.ds(i * rows, rows)
        held[at, :] = dot(pick, grads_ref[...]).astype(held.dtype)
        copy = pltpu.make_async_copy(held.at[at], out_ref.at[0, 0, at], sems.at[i])
        copy.start()
        copies.append(copy)
    for copy in copies:
        copy.wait()
    layer.wait()


def layer_kernel(
    n,
    tabs,
    dests,
    slots,
    lengths,
    tiles,
    ids_ref,
    table_ref,
    w_in_ref,
    w_out_ref,
    og_in_ref,
    out_ref,
    grads_ref,
    xg,
    dg,
    vqk,
    gq,
    pk,
    gk,
    pre,
    attn,
    seq,
    dq,
    dk,
    dv,
    dup,
    dm,
    up,
    xhat,
    xinv,
    startq,
    startk,
    route_out,
    route_in,
    back_out,
    back_in,
    xs,
    xr,
    ds_,
    dr,
    rs,
    rr,
    bs,
    br,
    held,
    w_in,
    w_out,
    looked,
    og_ref,
    local_sems,
):
    me = lax.axis_index("ctx")
    tab = lax.axis_index("tab")
    levels = n // FAST
    z = me // FAST
    x = me % FAST
    rows, width = looked.shape
    half = rows // 2
    per_half = half // BROWS
    hd = width // H
    scale = hd ** (-0.5)

    pieces = local_sems.shape[0] - 3
    piece = held.shape[0] // pieces
    loads = [
        pltpu.make_async_copy(
            table_ref.at[0, 0, pl.ds(i * piece, piece)],
            held.at[pl.ds(i * piece, piece)],
            local_sems.at[i],
        )
        for i in range(pieces)
    ]
    load_out = pltpu.make_async_copy(w_out_ref, w_out, local_sems.at[pieces])
    load_in = pltpu.make_async_copy(w_in_ref, w_in, local_sems.at[pieces + 1])
    for load in loads:
        load.start()
    load_out.start()
    load_og = pltpu.make_async_copy(og_in_ref, og_ref, local_sems.at[pieces + 2])
    load_og.start()
    load_in.start()

    barrier = pltpu.get_barrier_semaphore()

    def greet_ctx(k, carry):
        pl.semaphore_signal(
            barrier, inc=1, device_id=(lax.rem(me + k, n), tab), device_id_type=MESH
        )
        return carry

    def greet_tab(k, carry):
        pl.semaphore_signal(
            barrier, inc=1, device_id=(me, lax.rem(tab + k, tabs)), device_id_type=MESH
        )
        return carry

    lax.fori_loop(1, n, greet_ctx, 0)
    lax.fori_loop(1, tabs, greet_tab, 0)

    line = jnp.broadcast_to(ids_ref[0], (rows, rows))
    at_row = lax.broadcasted_iota(jnp.int32, (rows, rows), 0)
    at_lane = lax.broadcasted_iota(jnp.int32, (rows, rows), 1)
    column = jnp.where(at_row == at_lane, line, 0).astype(jnp.float32)
    column = jnp.sum(column, axis=1, keepdims=True)
    column = jnp.broadcast_to(column, (rows, 128)).astype(jnp.int32)
    lane = lax.broadcasted_iota(jnp.int32, (rows, 128), 1)
    found = jnp.zeros((rows, width), jnp.float32)
    for i, load in enumerate(loads):
        load.wait()
        picks = [
            jnp.where(column == lane + (i * piece + k * 128), 1.0, 0.0)
            for k in range(piece // 128)
        ]
        pick = jnp.concatenate(picks, axis=1).astype(jnp.bfloat16)
        found += dot(pick, held[pl.ds(i * piece, piece), :])
    looked[...] = found.astype(jnp.bfloat16)

    def choose(hit, block, other):
        on = jnp.full(block.shape, hit.astype(jnp.int32)) > 0
        return jnp.where(on, block, other)

    def block_for(t):
        block = looked[0:BROWS, :]
        for p in range(1, NBLK):
            other = looked[p * BROWS : (p + 1) * BROWS, :]
            block = choose(dests[0, tab, p] == t, other, block)
        return block

    def route_copy(src, dst, send, recv, t):
        return pltpu.make_async_remote_copy(
            src_ref=src.at[t],
            dst_ref=dst.at[tab],
            send_sem=send.at[t],
            recv_sem=recv.at[tab],
            device_id=(me, t),
            device_id_type=MESH,
        )

    def route_wait(src, dst, send, recv, t):
        pltpu.make_async_remote_copy(
            src_ref=src.at[t],
            dst_ref=dst.at[t],
            send_sem=send.at[t],
            recv_sem=recv.at[t],
            device_id=(me, t),
            device_id_type=MESH,
        ).wait()

    for k in range(tabs):
        t = lax.rem(tab + k, tabs)
        if k == 0:
            route_in[tab] = block_for(t)
        else:
            route_out[t] = block_for(t)

    pl.semaphore_wait(barrier, n + tabs - 2)

    for k in range(1, tabs):
        route_copy(route_out, route_in, rs, rr, lax.rem(tab + k, tabs)).start()

    load_out.wait()
    load_og.wait()
    dm[...] = dot_nt(og_ref[0], w_out[...])

    def starts_of(pos):
        end = jnp.int32(0)
        start = jnp.zeros_like(pos)
        for e in range(lengths.shape[1]):
            end = end + lengths[0, e]
            start = jnp.where(pos >= end, end, start)
        return start

    def base_of(s, side):
        return (2 * n - 1 - s) * half if side else s * half

    for side in range(2):
        local = lax.broadcasted_iota(jnp.int32, (half, 128), 0)
        startq[side * half : (side + 1) * half, :] = starts_of(local + base_of(me, side))
    chunk = lax.broadcasted_iota(jnp.int32, (2 * n, half), 0)
    startk[...] = starts_of(
        chunk * half + lax.broadcasted_iota(jnp.int32, (2 * n, half), 1)
    )
    attn[...] = jnp.zeros_like(attn)

    def tile_rows(pick):
        lane = lax.broadcasted_iota(jnp.int32, (BROWS, half), 1)
        stripes = []
        for a in range(per_half):
            line = jnp.full((BROWS, half), pick(a, 0))
            for b in range(1, per_half):
                line = jnp.where(lane >= b * BROWS, pick(a, b), line)
            stripes.append(line)
        return jnp.concatenate(stripes, axis=0) > 0

    def query_mask(s, mine, theirs):
        at, to = base_of(me, mine), base_of(s, theirs)
        own = lax.broadcasted_iota(jnp.int32, (half, half), 0) + at
        other = lax.broadcasted_iota(jnp.int32, (half, half), 1) + to
        first = startq[mine * half : (mine + 1) * half, :]
        at, to = at // BROWS, to // BROWS
        on = tile_rows(lambda a, b: tiles[0, at + a, to + b])
        return jnp.where((other <= own) & (other >= first) & on, 1.0, 0.0)

    def key_mask(s, mine, theirs):
        at, to = base_of(me, mine), base_of(s, theirs)
        own = lax.broadcasted_iota(jnp.int32, (half, half), 0) + at
        other = lax.broadcasted_iota(jnp.int32, (half, half), 1) + to
        first = startk[pl.ds(to // half, 1), :]
        at, to = at // BROWS, to // BROWS
        on = tile_rows(lambda a, b: tiles[0, to + b, at + a])
        return jnp.where((own <= other) & (own >= first) & on, 1.0, 0.0)

    def side_rows(side):
        return slice(side * half, (side + 1) * half)

    def take(part, s, side, h):
        return vqk[part, s, side_rows(side), h * hd : (h + 1) * hd]

    def project(s):
        block = xg[s]
        for part in range(3):
            lo = (part + 1) * width
            value = dot(block, w_in[:, lo : lo + width])
            vqk[part, s] = silu_half(0.5 * value).astype(jnp.bfloat16)

    def quads(s):
        return (
            (s <= me, 0, 0, 1, 1),
            (s >= n - 1 - me, 1, 0, 0, 1),
            (s >= me, 1, 1, 0, 0),
        )

    def scores(q, k, mask, halved):
        halfs = dot_nt(q, k) * (0.5 * scale)
        grown = 1.0 + jnp.tanh(halfs)
        value = halfs * grown
        slope = grown + value * (2.0 - grown)
        return (value * mask).astype(jnp.bfloat16), (slope * halved).astype(jnp.bfloat16)

    def key_forward(s):
        for i, (when, _, _, km, qt) in enumerate(quads(s)):

            @pl.when(when)
            def _(i=i, km=km, qt=qt):
                mask = key_mask(s, km, qt)
                halved = mask * (0.5 * scale)
                for h in range(H):
                    pk[i, s, h], gk[i, s, h] = scores(
                        take(2, me, km, h), take(1, s, qt, h), mask, halved
                    )

    def forward(s, both):
        project(s)
        for i, (when, qm, kt, km, qt) in enumerate(quads(s)):

            @pl.when(when)
            def _(i=i, qm=qm, kt=kt, km=km, qt=qt):
                mask = query_mask(s, qm, kt)
                halved = mask * (0.5 * scale)
                if both:
                    mask_k = key_mask(s, km, qt)
                    halved_k = mask_k * (0.5 * scale)
                for h in range(H):
                    cut = slice(h * hd, (h + 1) * hd)
                    probs, gq[i, s, h] = scores(
                        take(1, me, qm, h), take(2, s, kt, h), mask, halved
                    )
                    attn[side_rows(qm), cut] += dot(probs, take(0, s, kt, h))
                    if both:
                        pk[i, s, h], gk[i, s, h] = scores(
                            take(2, me, km, h), take(1, s, qt, h), mask_k, halved_k
                        )

    def query_back(s):
        for i, (when, qm, kt, _, _) in enumerate(quads(s)):

            @pl.when(when)
            def _(i=i, qm=qm, kt=kt):
                for h in range(H):
                    cut = slice(h * hd, (h + 1) * hd)
                    slope = gq[i, s, h].astype(jnp.float32)
                    dsc = dot_nt(dg[me, side_rows(qm), cut], take(0, s, kt, h)) * slope
                    dq[side_rows(qm), cut] += dot(
                        dsc.astype(jnp.bfloat16), take(2, s, kt, h)
                    )

    def key_back(s, _):
        for i, (when, _, _, km, qt) in enumerate(quads(s)):

            @pl.when(when)
            def _(i=i, km=km, qt=qt):
                for h in range(H):
                    cut = slice(h * hd, (h + 1) * hd)
                    grad = dg[s, side_rows(qt), cut]
                    slope = gk[i, s, h].astype(jnp.float32)
                    dsc = dot_nt(take(0, me, km, h), grad) * slope
                    dk[side_rows(km), cut] += dot(
                        dsc.astype(jnp.bfloat16), take(1, s, qt, h)
                    )
                    dv[side_rows(km), cut] += dot(pk[i, s, h], grad)

    def level(k, i):
        zz = z + jnp.where(i == 0, -k, k)
        there = (k >= 0) & (k < levels) & (zz >= 0) & (zz < levels)
        return zz, there & ((k > 0) | (i == 0))

    def gather(buf, send, recv, wanted, needed, compute, filler):
        partner = z * FAST + (FAST - 1 - x)

        def copy(s, side, way):
            to = (me - FAST, me + FAST, partner)[way]
            at = pl.ds(side * half, half)
            return pltpu.make_async_remote_copy(
                src_ref=buf.at[s, at],
                dst_ref=buf.at[s, at],
                send_sem=send.at[way, side, s],
                recv_sem=recv.at[side, s],
                device_id=(to, tab),
                device_id_type=MESH,
            )

        def ways(zz, side, action):
            s = zz * FAST + x

            @pl.when((zz >= z) & (z > 0) & wanted(0, s, side, z))
            def _():
                action(copy(s, side, 0))

            @pl.when((zz <= z) & (z < levels - 1) & wanted(1, s, side, z))
            def _():
                action(copy(s, side, 1))

            @pl.when(needed(partner, s, side))
            def _():
                action(copy(s, side, 2))

        def step(k, carry):
            for i in range(2):
                zz, there = level(k, i)

                @pl.when(there)
                def _(i=i, zz=zz):
                    s = zz * FAST + x
                    for side in range(2):
                        got = wanted(1, s, side, z - 1) if i == 0 else wanted(0, s, side, z + 1)

                        @pl.when((k > 0) & got)
                        def _(side=side):
                            copy(s, side, 2).wait_recv()

                        ways(zz, side, lambda c: c.start())

            filler(k)

            def own_column(i, carry):
                zz, there = level(k, i)

                @pl.when(there)
                def _():
                    compute(zz * FAST + x, True)

                return carry

            def other_column(i, carry):
                zz, there = level(k - 1, i)

                @pl.when(there)
                def _():
                    s = zz * FAST + (FAST - 1 - x)
                    for side in range(2):

                        @pl.when(needed(me, s, side))
                        def _(side=side):
                            copy(s, side, 2).wait_recv()

                    compute(s, False)

                return carry

            lax.fori_loop(0, 2, own_column, 0)
            lax.fori_loop(0, 2, other_column, 0)
            return carry

        lax.fori_loop(0, levels + 1, step, 0)

        def drain(zz, carry):
            for side in range(2):
                ways(zz, side, lambda c: c.wait_send())
            return carry

        lax.fori_loop(0, levels, drain, 0)

    load_in.wait()
    for k in range(1, tabs):
        route_wait(route_out, route_in, rs, rr, lax.rem(tab + k, tabs))

    def arrives(s, t):
        count = jnp.int32(0)
        for p in range(NBLK):
            hit = (dests[0, t, p] == tab) & (slots[0, t, p] == s)
            count += hit.astype(jnp.int32)
        return count > 0

    for s in range(NBLK):
        block = route_in[0]
        for t in range(1, tabs):
            block = choose(arrives(s, t), route_in[t], block)
        seq[s * BROWS : (s + 1) * BROWS, :] = block

    normal, inverse = layer_statistics(seq[...].astype(jnp.float32))
    xg[me] = normal.astype(jnp.bfloat16)
    xhat[...] = normal
    xinv[...] = jnp.broadcast_to(inverse, xinv.shape)

    def part_of(part):
        return w_in[:, part * width : (part + 1) * width]

    def own_rows(j):
        @pl.when(j == 0)
        def _():
            for part in range(4):
                halfs = 0.5 * dot(xg[me], part_of(part))
                tanh = jnp.tanh(halfs)
                pre[part] = slope_half(halfs, tanh)
                if part == 0:
                    act = (halfs * (1.0 + tanh)).astype(jnp.bfloat16)
                    up[...] = act.astype(jnp.float32)

    def always(*_):
        return me >= 0

    gather(xg, xs, xr, always, always, forward, own_rows)

    attn_hat, attn_inverse = layer_statistics(attn[...])
    dg[me] = norm_backward_pass(dm[...] * up[...], attn_hat, attn_inverse).astype(
        jnp.bfloat16
    )
    attn[...] = attn_hat
    dq[...] = jnp.zeros_like(dq)
    dk[...] = jnp.zeros_like(dk)
    dv[...] = jnp.zeros_like(dv)

    def d_pre(part, grad):
        return dot_nt((grad * pre[part]).astype(jnp.bfloat16), part_of(part))

    def own_back(j):
        @pl.when(j == 0)
        def _():
            attn_hat = attn[...]
            mixed = (attn_hat * up[...]).astype(jnp.bfloat16)
            out_ref[0] = (seq[...].astype(jnp.float32) + dot(mixed, w_out[...])).astype(
                jnp.bfloat16
            )
            dup[...] = d_pre(0, dm[...] * attn_hat)

        @pl.when(j < levels)
        def _():
            def one(i, carry):
                query_back(j * FAST + i)
                return carry

            lax.fori_loop(0, FAST, one, 0)

        def two(i, carry):
            zz, there = level(j - 1, i)

            @pl.when(there)
            def _():
                key_forward(zz * FAST + (FAST - 1 - x))

            return carry

        lax.fori_loop(0, 2, two, 0)

        @pl.when(j == levels)
        def _():
            dup[...] += d_pre(2, dq[...])

    def needed(d, s, side):
        if side == 0:
            return d <= s
        return (s <= d) | (s >= n - 1 - d)

    def wanted(way, s, side, at):
        if side == 0:
            return me >= 0 if way == 0 else me < 0
        return n - 1 - s <= at * FAST - 1 if way == 0 else me >= 0

    gather(dg, ds_, dr, wanted, needed, key_back, own_back)

    normalized = dup[...] + d_pre(1, dv[...]) + d_pre(3, dk[...])
    attn[...] = og_ref[0].astype(jnp.float32) + norm_backward_pass(
        normalized, xhat[...], xinv[:, 0:1]
    )

    def back_block(t):
        block = attn[0:BROWS, :]
        for s in range(1, NBLK):
            other = attn[s * BROWS : (s + 1) * BROWS, :]
            block = choose(arrives(s, t), other, block)
        return block.astype(jnp.bfloat16)

    for k in range(tabs):
        t = lax.rem(tab + k, tabs)
        if k == 0:
            back_in[tab] = back_block(t)
        else:
            back_out[t] = back_block(t)
            route_copy(back_out, back_in, bs, br, t).start()
    for k in range(1, tabs):
        route_wait(back_out, back_in, bs, br, lax.rem(tab + k, tabs))
    for p in range(NBLK):
        block = back_in[0]
        for t in range(1, tabs):
            block = choose(dests[0, tab, p] == t, back_in[t], block)
        grads_ref[p * BROWS : (p + 1) * BROWS, :] = block


def body(n, tabs, table, row_ids, dests, slots, lengths, tile_mask, w_in, w_out, og):
    count = row_ids.shape[2]
    width = w_out.shape[0]
    table_rows = table.shape[2]
    pieces = 8
    bf16, f32 = jnp.bfloat16, jnp.float32
    vmem = pl.BlockSpec(memory_space=pltpu.VMEM)
    smem = pl.BlockSpec(memory_space=pltpu.SMEM)
    hbm = pl.BlockSpec(memory_space=pl.ANY)
    dma = pltpu.SemaphoreType.DMA
    layer_out, row_grads = pl.pallas_call(
        functools.partial(layer_kernel, n, tabs),
        out_shape=(
            jax.ShapeDtypeStruct((1, count, width), bf16),
            jax.ShapeDtypeStruct((count, width), bf16),
        ),
        in_specs=[smem] * 4 + [vmem, hbm, hbm, hbm, hbm],
        out_specs=(vmem, vmem),
        scratch_shapes=[
            pltpu.VMEM((n, count, width), bf16),
            pltpu.VMEM((n, count, width), bf16),
            pltpu.VMEM((3, n, count, width), bf16),
            pltpu.VMEM((3, n, H, count // 2, count // 2), bf16),
            pltpu.VMEM((3, n, H, count // 2, count // 2), bf16),
            pltpu.VMEM((3, n, H, count // 2, count // 2), bf16),
            pltpu.VMEM((4, count, width), f32),
            pltpu.VMEM((count, width), f32),
            pltpu.VMEM((count, width), bf16),
            pltpu.VMEM((count, width), f32),
            pltpu.VMEM((count, width), f32),
            pltpu.VMEM((count, width), f32),
            pltpu.VMEM((count, width), f32),
            pltpu.VMEM((count, width), f32),
            pltpu.VMEM((count, width), f32),
            pltpu.VMEM((count, width), f32),
            pltpu.VMEM((count, 128), f32),
            pltpu.VMEM((count, 128), jnp.int32),
            pltpu.VMEM((2 * n, count // 2), jnp.int32),
            pltpu.VMEM((tabs, BROWS, width), bf16),
            pltpu.VMEM((tabs, BROWS, width), bf16),
            pltpu.VMEM((tabs, BROWS, width), bf16),
            pltpu.VMEM((tabs, BROWS, width), bf16),
            dma((3, 2, n)),
            dma((2, n)),
            dma((3, 2, n)),
            dma((2, n)),
            dma((tabs,)),
            dma((tabs,)),
            dma((tabs,)),
            dma((tabs,)),
            pltpu.VMEM((table_rows, width), bf16),
            pltpu.VMEM(w_in.shape, bf16),
            pltpu.VMEM(w_out.shape, bf16),
            pltpu.VMEM((count, width), bf16),
            pltpu.VMEM(og.shape, bf16),
            dma((pieces + 3,)),
        ],
        compiler_params=pltpu.CompilerParams(
            collective_id=0, has_side_effects=True, vmem_limit_bytes=60 * 1024 * 1024
        ),
        name="layer",
    )(dests, slots, lengths, tile_mask, row_ids, table, w_in, w_out, og)
    table_grad, layer_out = pl.pallas_call(
        scatter_kernel,
        out_shape=(
            jax.ShapeDtypeStruct((1, 1, table_rows, width), bf16),
            jax.ShapeDtypeStruct((1, count, width), bf16),
        ),
        in_specs=[vmem, vmem, vmem],
        out_specs=(hbm, hbm),
        scratch_shapes=[pltpu.VMEM((table_rows, width), bf16), dma((pieces + 1,))],
        name="table_grad",
    )(row_ids, row_grads, layer_out)
    return layer_out, table_grad


def solution(mesh):
    in_specs = (
        P("ctx", "tab", None, None),
        P("ctx", "tab", None),
        P("ctx", None, None),
        P("ctx", None, None),
        P("tab", None),
        P("tab", None, None),
        P(),
        P(),
        P("tab", "ctx", None),
    )
    out_specs = (P("tab", "ctx", None), P("ctx", "tab", None, None))
    return jax.shard_map(
        functools.partial(body, mesh.shape["ctx"], mesh.shape["tab"]),
        mesh=mesh,
        in_specs=in_specs,
        out_specs=out_specs,
        check_vma=False,
    )
```
